128 devices in a mesh: grp: 4 (over z), dom: 32 (over x, y, core).
Axes of the slice: x: 4, y: 4, z: 4, core: 2. Of those that a mesh axis runs over, the one named last changes fastest.
Arguments:
- operator_blocks: float32 [512, 16, 4096], P(('grp', 'dom')), may hold values from -0.75 to 0.75
- operator_cols: int32 [512, 16], P(('grp', 'dom')), may hold values from 0 to 31, as said below
- halo_count: int32 [512], P(('grp', 'dom')), may hold values from 2 to 4, as said below
- prolong_blocks: float32 [512, 8, 4096], P(('grp', 'dom')), may hold values from -0.75 to 0.75
- prolong_cols: int32 [512, 8], P(('grp', 'dom')), may hold values from 0 to 255, as said below
- prolong_slot: int32 [512, 8], P(('grp', 'dom')), may hold values from 0 to 63, as said below
- send_lists: int32 [128, 32], P(('grp', 'dom')), may hold values from 0 to 3
- slot_owner_row: int32 [128, 64], P(('grp', 'dom')), may hold values from 0 to 2, as said below
- coarse_pattern: int32 [256, 16], P(('grp', 'dom')), may hold values from 0 to 255, as said below
Outputs:
- coarse_blocks: float32 [256, 16, 4096], P(('grp', 'dom'))
The draws below stay inside these ranges and needn't reach their ends.
Inputs may be any that keep to these rules, and one draw needn't show every extreme that they name: `operator_cols`: slots below 12 hold values below 16, the others values below 32. Slots at or beyond a row's live count hold valid values whose blocks do not count. `halo_count`: the first fine row of every device has 4. `prolong_cols`: the 8 values of a row are different. A row on grp index g names coarse rows owned by devices of grp index g only. Slot t of device v stands for owner dom index t // 2 and owner coarse row slot_owner_row[v, t]; prolong_cols[i, j] = ((v // 32) * 32 + s // 2) * 2 + slot_owner_row[v, s] for s = prolong_slot[i, j]; the slots of a row are different and never empty. `slot_owner_row`: the value 2 marks an empty slot; the live values of one device for one owner are different; every device fills all 2 slots of its own dom index and the first slot of every owner, and no other slot. `coarse_pattern`: the 16 values of a row are different.
All inputs are finite; a program needn't handle non-finite values.
Results may differ from the reference program's by a relative error of at most 0.0003.
Values sent between devices are 32-bit elements; how exact they have to be, the bound alone decides.
No kernel may reach another device: no remote copies, remote signals or barrier semaphores. Data moves between devices by JAX's collectives and lax.ppermute only.
A program may use at most 128 MiB of HBM per device.

```python
import jax
import jax.numpy as jnp
from jax import lax

BS = 64
RB = 4
CB = 2
KG = 12
KH = 4
KA = 16
KP = 8
KC = 16
HS = 1
CAP = 2
ROWS = 512
NC = 256
N_GRP = 4
N_DOM = 32


def common_draw(key):
    devices_all = N_GRP * N_DOM
    slot_total = N_DOM * CAP
    far_total = N_DOM * HS
    score = jax.random.randint(jax.random.fold_in(key, 1), (devices_all, N_DOM, CB), 0, 1 << 20) * CB + jnp.arange(CB, dtype=jnp.int32)
    order = jnp.argsort(score, axis=-1)[..., :CAP].astype(jnp.int32)
    own_domain = (jnp.arange(N_DOM, dtype=jnp.int32)[None, :] == (jnp.arange(devices_all, dtype=jnp.int32) % N_DOM)[:, None])[..., None]
    first_slot = (jnp.arange(CAP, dtype=jnp.int32) == 0)[None, None, :]
    live_slot = own_domain | first_slot
    owner_row = jnp.where(live_slot, order, CB).reshape(devices_all, slot_total).astype(jnp.int32)
    live_flat = live_slot.reshape(devices_all, slot_total)
    pick_score = jax.random.randint(jax.random.fold_in(key, 3), (devices_all, RB, slot_total), 0, 1 << 20) * slot_total + jnp.arange(slot_total, dtype=jnp.int32)
    pick_score = jnp.where(live_flat[:, None, :], pick_score, -1)
    chosen = lax.top_k(pick_score, KP)[1].astype(jnp.int32)
    chosen_rows = jnp.take_along_axis(jnp.broadcast_to(owner_row[:, None, :], (devices_all, RB, slot_total)), chosen, axis=2)
    group_of = jnp.arange(devices_all, dtype=jnp.int32) // N_DOM
    prolong_cols = ((group_of[:, None, None] * N_DOM + chosen // CAP) * CB + chosen_rows).reshape(ROWS, KP).astype(jnp.int32)
    prolong_slot = chosen.reshape(ROWS, KP)
    send_lists = jax.random.randint(jax.random.fold_in(key, 4), (devices_all, N_DOM * HS), 0, RB).astype(jnp.int32)
    near_part = jax.random.randint(jax.random.fold_in(key, 5), (ROWS, KG), 0, N_GRP * RB)
    far_score = jax.random.randint(jax.random.fold_in(key, 6), (devices_all, far_total), 0, 1 << 20) * far_total + jnp.arange(far_total, dtype=jnp.int32)
    far_perm = jnp.argsort(far_score, axis=-1).astype(jnp.int32)
    position = (jnp.arange(KH, dtype=jnp.int32)[None, :] * RB + jnp.arange(RB, dtype=jnp.int32)[:, None]) % far_total
    far_part = jnp.take_along_axis(jnp.broadcast_to(far_perm[:, None, :], (devices_all, RB, far_total)), jnp.broadcast_to(position[None], (devices_all, RB, KH)), axis=2).reshape(ROWS, KH)
    operator_cols = jnp.concatenate([near_part, far_part], axis=1).astype(jnp.int32)
    random_count = jax.random.randint(jax.random.fold_in(key, 7), (ROWS,), 2, KH + 1)
    halo_count = jnp.where(jnp.arange(ROWS, dtype=jnp.int32) % RB == 0, KH, random_count).astype(jnp.int32)
    row_index = jnp.arange(ROWS, dtype=jnp.int32)
    device = row_index // RB
    domain = device % N_DOM
    near_rows = (near_part // RB * N_DOM + domain[:, None]) * RB + near_part % RB
    source = (device // N_DOM)[:, None] * N_DOM + far_part // HS
    far_rows = source * RB + send_lists[source, domain[:, None] * HS + far_part % HS]
    columns = jnp.concatenate([near_rows, far_rows], axis=1)
    live_far = (jnp.arange(KH, dtype=jnp.int32)[None, :] < halo_count[:, None]).astype(jnp.int32)
    live_all = jnp.concatenate([jnp.ones((ROWS, KG), jnp.int32), live_far], axis=1)
    expanded = prolong_cols[columns]
    flat_pair = prolong_cols[:, :, None, None] * NC + expanded[:, None, :, :]
    weight_pair = jnp.broadcast_to(live_all[:, None, :, None], flat_pair.shape)
    counts = jnp.zeros((NC * NC,), jnp.int32).at[flat_pair.reshape(-1)].add(weight_pair.reshape(-1)).reshape(NC, NC)
    tie_break = jax.random.randint(jax.random.fold_in(key, 8), (NC, NC), 0, 1 << 10) * NC + jnp.arange(NC, dtype=jnp.int32)[None, :]
    coarse_pattern = lax.top_k(counts * (NC << 10) + tie_break, KC)[1].astype(jnp.int32)
    return (operator_cols, halo_count, prolong_cols, prolong_slot, send_lists, owner_row, coarse_pattern)


def draw_operator_cols(key, part):
    return common_draw(jax.random.fold_in(key, 77))[0]


def draw_halo_count(key, part):
    return common_draw(jax.random.fold_in(key, 77))[1]


def draw_prolong_cols(key, part):
    return common_draw(jax.random.fold_in(key, 77))[2]


def draw_prolong_slot(key, part):
    return common_draw(jax.random.fold_in(key, 77))[3]


def draw_send_lists(key, part):
    return common_draw(jax.random.fold_in(key, 77))[4]


def draw_slot_owner_row(key, part):
    return common_draw(jax.random.fold_in(key, 77))[5]


def draw_coarse_pattern(key, part):
    return common_draw(jax.random.fold_in(key, 77))[6]


def level_of(stream_key, shape, split, low, largest):
    loudness = 1.0
    for dim, parts in split:
        draws = jax.random.uniform(jax.random.fold_in(jax.random.fold_in(stream_key, 6), dim), (parts,), jnp.float32, low / len(split), largest / len(split))
        loudness = loudness * jnp.repeat(jnp.exp(draws), shape[dim] // parts).reshape((-1,) + (1,) * (len(shape) - 1 - dim))
    return loudness


def scatter_about(stream_key, shape, spread, bound, split=(), held_as=jnp.bfloat16):
    array = jax.random.normal(stream_key, shape, jnp.float32) * spread
    if len(split) > 0:
        array = level_of(stream_key, shape, split, -0.22, 0.18) * array
    return jnp.clip(array, min=-bound, max=bound).astype(held_as)


def setup_inputs(seed: int = 0) -> dict:
    splits = jax.random.split(jax.random.key(seed), 10)
    return {
        "operator_blocks": scatter_about(splits[0], (ROWS, KA, BS * BS), BS ** -0.5, 0.75, ((0, 128),), jnp.float32),
        "operator_cols": draw_operator_cols(jax.random.fold_in(splits[9], 71), 0),
        "halo_count": draw_halo_count(jax.random.fold_in(splits[9], 71), 0),
        "prolong_blocks": scatter_about(splits[3], (ROWS, KP, BS * BS), BS ** -0.5, 0.75, ((0, 128),), jnp.float32),
        "prolong_cols": draw_prolong_cols(jax.random.fold_in(splits[9], 71), 0),
        "prolong_slot": draw_prolong_slot(jax.random.fold_in(splits[9], 71), 0),
        "send_lists": draw_send_lists(jax.random.fold_in(splits[9], 71), 0),
        "slot_owner_row": draw_slot_owner_row(jax.random.fold_in(splits[9], 71), 0),
        "coarse_pattern": draw_coarse_pattern(jax.random.fold_in(splits[9], 71), 0),
    }


EXACT = lax.Precision.HIGHEST


def column_map(operator_cols, send_lists):
    row_index = jnp.arange(ROWS, dtype=jnp.int32)
    device = row_index // RB
    group_index = device // N_DOM
    domain = device % N_DOM
    near_slots = operator_cols[:, :KG]
    near_rows = ((near_slots // RB) * N_DOM + domain[:, None]) * RB + near_slots % RB
    far_slots = operator_cols[:, KG:]
    source = group_index[:, None] * N_DOM + far_slots // HS
    far_rows = source * RB + send_lists[source, domain[:, None] * HS + far_slots % HS]
    return jnp.concatenate([near_rows, far_rows], axis=1).astype(jnp.int32)


def live_mask(halo_count):
    near_live = jnp.ones((halo_count.shape[0], KG), jnp.float32)
    far_live = (jnp.arange(KH, dtype=jnp.int32)[None, :] < halo_count[:, None]).astype(jnp.float32)
    return jnp.concatenate([near_live, far_live], axis=1)


def target_rows(prolong_slot, slot_owner_row):
    device = jnp.arange(ROWS, dtype=jnp.int32) // RB
    owner_row = slot_owner_row[device[:, None], prolong_slot]
    return (((device // N_DOM)[:, None] * N_DOM + prolong_slot // CAP) * CB + owner_row).astype(jnp.int32)


def reference(operator_blocks, operator_cols, halo_count, prolong_blocks, prolong_cols, prolong_slot, send_lists, slot_owner_row, coarse_pattern):
    columns = column_map(operator_cols, send_lists)
    live_slots = jnp.repeat(live_mask(halo_count), KP, axis=1)
    expanded_ids = prolong_cols[columns].reshape(ROWS, KA * KP)
    target_ids = target_rows(prolong_slot, slot_owner_row)
    block_count = ROWS // RB
    square = prolong_blocks.reshape(ROWS, KP, BS, BS)
    blocks = (operator_blocks.reshape(block_count, RB, KA, BS, BS), columns.reshape(block_count, RB, KA),
              expanded_ids.reshape(block_count, RB, KA * KP), live_slots.reshape(block_count, RB, KA * KP),
              square.reshape(block_count, RB, KP, BS, BS), target_ids.reshape(block_count, RB, KP))

    def add_block(coarse_sum, pieces):
        operator, columns_block, coarse_ids, live_block, panels, targets = pieces
        fetched = square[columns_block]
        weights = jnp.einsum('rmax,rmqxd->rmqad', operator, fetched, precision=EXACT).reshape(RB, KA * KP, BS * BS)
        wanted = coarse_pattern[targets]
        select = (wanted[..., None] == coarse_ids[:, None, None, :]).astype(jnp.float32) * live_block[:, None, None, :]
        matched = jnp.einsum('rjce,rex->rjcx', select, weights, precision=EXACT).reshape(RB, KP, KC, BS, BS)
        pair_terms = jnp.einsum('rjab,rjcad->rjcbd', panels, matched, precision=EXACT)
        return coarse_sum.at[targets.reshape(RB * KP)].add(pair_terms.reshape(RB * KP, KC, BS * BS)), None

    start = jnp.zeros((NC, KC, BS * BS), jnp.float32)
    return lax.scan(add_block, start, blocks)[0]
```

```python
import functools

import jax
import jax.numpy as jnp
from jax import lax
from jax.experimental import pallas as pl
from jax.experimental.pallas import tpu as pltpu
from jax.sharding import PartitionSpec as P

BS = 64
KG = 12
KH = 4
KA = 16
KP = 8
KC = 16
RB = 4
PAIRS = RB * KP
NEAR_E = KG * KP
FAR_E = KH * KP
LANES = 128
ROW_T = KP * BS * BS // LANES


def split(x):
    hi = x.astype(jnp.bfloat16)
    lo = (x - hi.astype(jnp.float32)).astype(jnp.bfloat16)
    return hi, lo


def paired(blocks):
    rows, n, _ = blocks.shape
    view = blocks.reshape(rows, n // 2, 2, BS, BS)
    return view.transpose(0, 1, 3, 2, 4).reshape(rows, n // 2, BS, LANES)


def put_right(right_ref, slot, table):
    for s in range(4):
        hi, lo = split(table(s))
        cols = slice(s * LANES, (s + 1) * LANES)
        right_ref[slot, 0:64, cols] = hi
        right_ref[slot, 64:128, cols] = hi
        right_ref[slot, 128:192, cols] = lo
        right_ref[slot, 192:256, cols] = lo


def left_of(pair):
    hi = pair.astype(jnp.bfloat16).astype(jnp.float32)
    lo = pltpu.roll(pair - hi, BS, axis=1)
    first = lax.broadcasted_iota(jnp.int32, pair.shape, 1) < BS
    even = jnp.where(first, hi, lo).astype(jnp.bfloat16)
    odd = jnp.where(first, lo, hi).astype(jnp.bfloat16)
    return jnp.concatenate([even, even], axis=1), jnp.concatenate([odd, odd], axis=1)


def add_matches(list_ref, base, count, w_ref, m_ref):
    half = lax.broadcasted_iota(jnp.int32, (BS, LANES), 1) // BS

    def body(k, carry):
        code = list_ref[base + k]
        e = code >> 4
        c = code & 15
        w = pltpu.roll(w_ref[e >> 1], ((e ^ c) & 1) * BS, axis=1)
        m_ref[c >> 1] += jnp.where(half == (c & 1), w, 0.0)
        return carry

    lax.fori_loop(0, count, body, 0)


def near_kernel(cols_ref, list_ref, count_ref, a_ref, p0, p1, p2, p3, m_ref, left_ref, right_ref, w_ref):
    i = pl.program_id(0)

    @pl.when(i == 0)
    def _():
        for k, ref in enumerate((p0, p1, p2, p3)):

            def put(r, carry, k=k, ref=ref):
                def table(s):
                    return ref[pl.ds(pl.multiple_of(r * ROW_T + s * BS, BS), BS), :]

                put_right(right_ref, k * RB + r, table)
                return carry

            lax.fori_loop(0, RB, put, 0)

    for s in range(4):
        slab = p0[pl.ds(pl.multiple_of(i * ROW_T + s * BS, BS), BS), :]
        hi = slab.astype(jnp.bfloat16).astype(jnp.float32)
        lo = slab - hi
        tall = jnp.concatenate([hi, hi, lo, lo], axis=0)
        left_ref[0, s * LANES : (s + 1) * LANES, :] = tall.T.astype(jnp.bfloat16)

    for pair in range(KG // 2):
        lefts = left_of(a_ref[0, pair])
        for t in range(2):
            m = 2 * pair + t
            col = cols_ref[i * KG + m]
            w = jnp.dot(lefts[t], right_ref[col], preferred_element_type=jnp.float32)
            for s in range(4):
                w_ref[m * 4 + s] = w[:, s * LANES : (s + 1) * LANES]

    def per_target(j, carry):
        m_ref[0, j] = jnp.zeros((KC // 2, BS, LANES), jnp.float32)
        add_matches(list_ref, (i * KP + j) * NEAR_E, count_ref[i * KP + j], w_ref, m_ref.at[0, j])
        return carry

    lax.fori_loop(0, KP, per_target, 0)


def far_kernel(
    cols_ref, list_ref, count_ref, pos_ref, a_ref, f0, f1, f2, f3, m_ref, left_ref,
    first_ref, second_ref, right_ref, w_ref, wide_ref, acc_ref, sems,
):
    i = pl.program_id(0)
    n_pos = acc_ref.shape[0]

    @pl.when(i == 0)
    def _():
        def clear(k, carry):
            acc_ref[k] = jnp.zeros(acc_ref.shape[1:], jnp.float32)
            return carry

        lax.fori_loop(0, n_pos, clear, 0)

    far = (f0, f1, f2, f3)
    for pair in range(KH // 2):
        lefts = left_of(a_ref[0, pair])
        for t in range(2):
            m = 2 * pair + t

            def table(s, m=m):
                return far[m][0, s * BS : (s + 1) * BS, :]

            put_right(right_ref, m, table)
            w = jnp.dot(lefts[t], right_ref[m], preferred_element_type=jnp.float32)
            for s in range(4):
                w_ref[m * 4 + s] = w[:, s * LANES : (s + 1) * LANES]

    def per_target(j, carry):
        here = i * KP + j
        add_matches(list_ref, here * FAR_E, count_ref[here], w_ref, m_ref.at[0, j])
        for s in range(KC // 2):
            hi, lo = split(m_ref[0, j, s])
            cols = slice(s * LANES, (s + 1) * LANES)
            wide_ref[0:64, cols] = hi
            wide_ref[64:128, cols] = lo
            wide_ref[128:192, cols] = hi
            wide_ref[192:256, cols] = lo
        left = left_ref[0, pl.ds(pl.multiple_of(j * BS, BS), BS), :]
        out = jnp.dot(left, wide_ref[...], preferred_element_type=jnp.float32)
        pos = pos_ref[here]
        for s in range(KC // 2):
            acc_ref[pos, s * BS : (s + 1) * BS, :] += out[:, s * LANES : (s + 1) * LANES]
        return carry

    lax.fori_loop(0, KP, per_target, 0)

    @pl.when(i == pl.num_programs(0) - 1)
    def _():
        a = pltpu.make_async_copy(acc_ref.at[pl.ds(0, n_pos - 1)], first_ref, sems.at[0])
        b = pltpu.make_async_copy(acc_ref.at[pl.ds(n_pos - 1, 1)], second_ref, sems.at[1])
        a.start()
        b.start()
        a.wait()
        b.wait()


def outgoing_kernel(pick_ref, p_ref, out_ref, sem):
    n = out_ref.shape[0]

    def copy(k):
        src = p_ref.at[pl.ds(pl.multiple_of(pick_ref[k] * ROW_T, ROW_T), ROW_T)]
        return pltpu.make_async_copy(src, out_ref.at[k], sem.at[k])

    def start(k, carry):
        copy(k).start()
        return carry

    def wait(k, carry):
        copy(k).wait()
        return carry

    lax.fori_loop(0, n, start, 0)
    lax.fori_loop(0, n, wait, 0)


def match_lists(wanted, ids, live):
    n = ids.shape[1]
    eq = wanted[:, :, None] == ids[:, None, :]
    c_of = jnp.sum(jnp.where(eq, jnp.arange(KC, dtype=jnp.int32)[None, :, None], 0), axis=1)
    hit = jnp.any(eq, axis=1) & live
    number = jnp.arange(n, dtype=jnp.int32)
    before = jnp.sum(jnp.where((number[:, None] < number[None, :])[None], hit[:, :, None].astype(jnp.int32), 0), axis=1)
    code = number[None, :] * KC + c_of
    here = hit[:, None, :] & (before[:, None, :] == number[None, :, None])
    lists = jnp.sum(jnp.where(here, code[:, None, :], 0), axis=2)
    return lists.reshape(-1), jnp.sum(hit.astype(jnp.int32), axis=1)


def pick_rows(table, index):
    n = table.shape[0]
    one = index[:, None] == jnp.arange(n, dtype=jnp.int32)[None, :]
    return jnp.sum(jnp.where(one[:, :, None], table[None], 0), axis=1)


def per_device(
    operator_blocks,
    operator_cols,
    halo_count,
    prolong_blocks,
    prolong_cols,
    prolong_slot,
    send_lists,
    slot_owner_row,
    coarse_pattern,
):
    n_dom = lax.axis_size("dom")
    n_grp = lax.axis_size("grp")
    g = lax.axis_index("grp")
    d = lax.axis_index("dom")
    owner = slot_owner_row.reshape(-1)

    panels = paired(prolong_blocks).reshape(RB * ROW_T, LANES)
    outgoing = pl.pallas_call(
        outgoing_kernel,
        out_shape=jax.ShapeDtypeStruct((n_dom, ROW_T, LANES), jnp.float32),
        grid_spec=pltpu.PrefetchScalarGridSpec(
            num_scalar_prefetch=1,
            grid=(1,),
            in_specs=[pl.BlockSpec(memory_space=pl.ANY)],
            out_specs=pl.BlockSpec(memory_space=pl.ANY),
            scratch_shapes=[pltpu.SemaphoreType.DMA((n_dom,))],
        ),
        name="outgoing",
    )(send_lists.reshape(-1), panels)
    far_rows = lax.all_to_all(outgoing, "dom", split_axis=0, concat_axis=0, tiled=True)

    id_tile = jnp.pad(prolong_cols.reshape(1, PAIRS).astype(jnp.float32), ((0, 7), (0, LANES - PAIRS)))
    carried = jnp.concatenate([panels, id_tile], axis=0)
    near_rows = [carried]
    for k in range(1, n_grp):
        near_rows.append(lax.ppermute(carried, "grp", [((z + k) % n_grp, z) for z in range(n_grp)]))

    mine = jnp.concatenate(
        [prolong_cols.reshape(-1), coarse_pattern.reshape(-1), send_lists.reshape(-1), owner.reshape(n_dom, 2)[:, 0]]
    )
    told = lax.all_to_all(
        jnp.broadcast_to(mine[None], (n_dom, mine.shape[0])), "dom", split_axis=0, concat_axis=0, tiled=True
    )
    all_cols = told[:, :PAIRS].reshape(n_dom, RB, KP)
    patterns = told[:, PAIRS : 2 * PAIRS].reshape(2 * n_dom, KC)
    here = jnp.arange(n_dom, dtype=jnp.int32)[None, :] == d
    picked = jnp.sum(jnp.where(here, told[:, 2 * PAIRS : 2 * PAIRS + n_dom], 0), axis=1)
    first_row = jnp.sum(jnp.where(here, told[:, 2 * PAIRS + n_dom :], 0), axis=1)
    far_ids = jnp.sum(
        jnp.where((picked[:, None] == jnp.arange(RB, dtype=jnp.int32))[:, :, None], all_cols, 0), axis=1
    )

    slots = prolong_slot.reshape(-1)
    slot_row = pick_rows(owner[:, None], slots)[:, 0]
    wanted = pick_rows(patterns, (slots // 2) * 2 + slot_row)
    position = jnp.where(slots % 2 == 1, n_dom, slots // 2)

    near_ids_table = jnp.concatenate(
        [rows[RB * ROW_T, :PAIRS].astype(jnp.int32).reshape(RB, KP) for rows in near_rows], axis=0
    )
    near_slots = operator_cols[:, :KG]
    near_cols = (((near_slots // RB) - g) % n_grp * RB + near_slots % RB).reshape(-1)
    far_cols = operator_cols[:, KG:].reshape(-1)
    near_ids = pick_rows(near_ids_table, near_cols).reshape(RB, NEAR_E)
    far_ids = pick_rows(far_ids, far_cols).reshape(RB, FAR_E)
    live = jnp.arange(KH, dtype=jnp.int32)[None, :] < halo_count[:, None]
    spread = lambda x: jnp.repeat(x, KP, axis=0)
    near_list, near_count = match_lists(wanted, spread(near_ids), jnp.ones((PAIRS, NEAR_E), bool))
    far_list, far_count = match_lists(wanted, spread(far_ids), spread(jnp.repeat(live, KP, axis=1)))

    operator = paired(operator_blocks)
    row_block = pl.BlockSpec((RB * ROW_T, LANES), lambda i, *_: (0, 0))
    matched, left = pl.pallas_call(
        near_kernel,
        out_shape=(
            jax.ShapeDtypeStruct((RB, KP, KC // 2, BS, LANES), jnp.float32),
            jax.ShapeDtypeStruct((RB, KP * BS, 256), jnp.bfloat16),
        ),
        grid_spec=pltpu.PrefetchScalarGridSpec(
            num_scalar_prefetch=3,
            grid=(RB,),
            in_specs=[pl.BlockSpec((1, KG // 2, BS, LANES), lambda i, *_: (i, 0, 0, 0))] + [row_block] * 4,
            out_specs=(
                pl.BlockSpec((1, KP, KC // 2, BS, LANES), lambda i, *_: (i, 0, 0, 0, 0)),
                pl.BlockSpec((1, KP * BS, 256), lambda i, *_: (i, 0, 0)),
            ),
            scratch_shapes=[
                pltpu.VMEM((4 * RB, 256, KP * BS), jnp.bfloat16),
                pltpu.VMEM((NEAR_E // 2, BS, LANES), jnp.float32),
            ],
        ),
        compiler_params=pltpu.CompilerParams(vmem_limit_bytes=40 * 2**20),
        cost_estimate=pl.CostEstimate(flops=10**10, bytes_accessed=16 * 2**20, transcendentals=0),
        name="near",
    )(near_cols, near_list, near_count, operator[:, : KG // 2], *near_rows)

    far_spec = lambda m: pl.BlockSpec((1, ROW_T, LANES), lambda i, cols, *_: (cols[i * KH + m], 0, 0))
    first, second = pl.pallas_call(
        far_kernel,
        out_shape=(
            jax.ShapeDtypeStruct((n_dom, KC // 2 * BS, LANES), jnp.float32),
            jax.ShapeDtypeStruct((1, KC // 2 * BS, LANES), jnp.float32),
        ),
        grid_spec=pltpu.PrefetchScalarGridSpec(
            num_scalar_prefetch=4,
            grid=(RB,),
            in_specs=[pl.BlockSpec((1, KH // 2, BS, LANES), lambda i, *_: (i, 0, 0, 0))]
            + [far_spec(m) for m in range(KH)]
            + [
                pl.BlockSpec((1, KP, KC // 2, BS, LANES), lambda i, *_: (i, 0, 0, 0, 0)),
                pl.BlockSpec((1, KP * BS, 256), lambda i, *_: (i, 0, 0)),
            ],
            out_specs=(pl.BlockSpec(memory_space=pl.ANY), pl.BlockSpec(memory_space=pl.ANY)),
            scratch_shapes=[
                pltpu.VMEM((KH, 256, KP * BS), jnp.bfloat16),
                pltpu.VMEM((FAR_E // 2, BS, LANES), jnp.float32),
                pltpu.VMEM((256, KC * BS), jnp.bfloat16),
                pltpu.VMEM((n_dom + 1, KC // 2 * BS, LANES), jnp.float32),
                pltpu.SemaphoreType.DMA((2,)),
            ],
        ),
        compiler_params=pltpu.CompilerParams(vmem_limit_bytes=40 * 2**20),
        cost_estimate=pl.CostEstimate(flops=10**10, bytes_accessed=24 * 2**20, transcendentals=0),
        name="far",
    )(far_cols, far_list, far_count, position, operator[:, KG // 2 :], *([far_rows] * KH), matched, left)

    arriving = lax.all_to_all(first, "dom", split_axis=0, concat_axis=0, tiled=True)
    own_first = jnp.sum(jnp.where(jnp.arange(2 * n_dom, dtype=jnp.int32) == 2 * d, owner, 0))
    rows = []
    for r in range(2):
        total = jnp.sum(jnp.where((first_row == r)[:, None, None], arriving, 0.0), axis=0)
        rows.append(total + jnp.where(own_first == r, 0.0, second[0]))
    coarse = jnp.stack(rows).reshape(2, KC // 2, BS, 2, BS)
    return coarse.transpose(0, 1, 3, 2, 4).reshape(2, KC, BS * BS)


def solution(mesh):
    return jax.shard_map(
        per_device,
        mesh=mesh,
        in_specs=(
            P(("grp", "dom"), None, None),
            P(("grp", "dom"), None),
            P(("grp", "dom")),
            P(("grp", "dom"), None, None),
            P(("grp", "dom"), None),
            P(("grp", "dom"), None),
            P(("grp", "dom"), None),
            P(("grp", "dom"), None),
            P(("grp", "dom"), None),
        ),
        out_specs=P(("grp", "dom"), None, None),
        check_vma=False,
    )
```

```python
import functools

import jax
import jax.numpy as jnp
from jax import lax
from jax.experimental import pallas as pl
from jax.experimental.pallas import tpu as pltpu
from jax.sharding import PartitionSpec as P

BS = 64
KG = 12
KH = 4
KA = 16
KP = 8
KC = 16
RB = 4
PAIRS = RB * KP
NEAR_E = KG * KP
FAR_E = KH * KP
LANES = 128
ROW_T = KP * BS * BS // LANES


def split(x):
    hi = x.astype(jnp.bfloat16)
    lo = (x - hi.astype(jnp.float32)).astype(jnp.bfloat16)
    return hi, lo


def paired(blocks):
    rows, n, _ = blocks.shape
    view = blocks.reshape(rows, n // 2, 2, BS, BS)
    return view.transpose(0, 1, 3, 2, 4).reshape(rows, n // 2, BS, LANES)


def first_half(shape):
    return lax.broadcasted_iota(jnp.int32, shape, 1) < BS


def put_right(right_ref, slot, table):
    for s in range(4):
        hi, lo = split(table(s))
        cols = slice(s * LANES, (s + 1) * LANES)
        right_ref[slot, 0:64, cols] = hi
        right_ref[slot, 64:128, cols] = hi
        right_ref[slot, 128:192, cols] = lo
        right_ref[slot, 192:256, cols] = lo


def spread_rows(a_ref, spread_ref):
    for t in range(a_ref.shape[1] // 8):
        for k in range(BS // 2):
            part = a_ref[0, t * 8 : (t + 1) * 8, k * LANES : (k + 1) * LANES]
            spread_ref[pl.ds(t * 8 * (BS // 2) + k, 8, stride=BS // 2), :] = part


def left_of(two):
    hi = two.astype(jnp.bfloat16).astype(jnp.float32)
    lo = pltpu.roll(two - hi, BS, axis=1)
    first = first_half(two.shape)
    rows = jnp.concatenate([jnp.where(first, hi, lo), jnp.where(first, lo, hi)], axis=0).astype(jnp.bfloat16)
    return jnp.concatenate([rows, rows], axis=1)


def add_matches(list_ref, base, count, w_ref, m_ref):
    half = lax.broadcasted_iota(jnp.int32, (BS, LANES), 1) // BS

    def body(k, carry):
        code = list_ref[base + k]
        e = code >> 4
        c = code & 15
        w = pltpu.roll(w_ref[e >> 1], ((e ^ c) & 1) * BS, axis=1)
        m_ref[c >> 1] += jnp.where(half == (c & 1), w, 0.0)
        return carry

    lax.fori_loop(0, count, body, 0)


def near_kernel(
    cols_ref, list_ref, count_ref, a_ref, p0, p1, p2, p3, m_ref, left_ref, right_ref, w_ref, spread_ref
):
    i = pl.program_id(0)

    @pl.when(i == 0)
    def _():
        for k, ref in enumerate((p0, p1, p2, p3)):

            def put(r, carry, k=k, ref=ref):
                def table(s):
                    return ref[pl.ds(pl.multiple_of(r * ROW_T + s * BS, BS), BS), :]

                put_right(right_ref, k * RB + r, table)
                return carry

            lax.fori_loop(0, RB, put, 0)

    for s in range(4):
        base = pl.multiple_of(i * ROW_T + s * BS, BS)
        slab = jnp.concatenate(
            [p0[pl.ds(base, BS // 2, stride=2), :], p0[pl.ds(base + 1, BS // 2, stride=2), :]], axis=0
        )
        hi = slab.astype(jnp.bfloat16).astype(jnp.float32)
        lo = slab - hi
        tall = jnp.concatenate([hi, hi, lo, lo], axis=0)
        left_ref[0, s * LANES : (s + 1) * LANES, :] = tall.T.astype(jnp.bfloat16)

    spread_rows(a_ref, spread_ref)
    for m in range(KG):
        left = left_of(spread_ref[m * (BS // 2) : (m + 1) * (BS // 2), :])
        w = jnp.dot(left, right_ref[cols_ref[i * KG + m]], preferred_element_type=jnp.float32)
        for s in range(4):
            w_ref[m * 4 + s] = w[:, s * LANES : (s + 1) * LANES]

    def per_target(j, carry):
        m_ref[0, j] = jnp.zeros((KC // 2, BS, LANES), jnp.float32)
        add_matches(list_ref, (i * KP + j) * NEAR_E, count_ref[i * KP + j], w_ref, m_ref.at[0, j])
        return carry

    lax.fori_loop(0, KP, per_target, 0)


def far_kernel(
    cols_ref, list_ref, count_ref, pos_ref, a_ref, f0, f1, f2, f3, m_ref, left_ref,
    out0, out1, out2, out3, out4, right_ref, w_ref, wide_ref, acc_ref, spread_ref, sems,
):
    i = pl.program_id(0)
    n_pos = acc_ref.shape[0]

    @pl.when(i == 0)
    def _():
        def clear(k, carry):
            acc_ref[k] = jnp.zeros(acc_ref.shape[1:], jnp.float32)
            return carry

        lax.fori_loop(0, n_pos, clear, 0)

    far = (f0, f1, f2, f3)
    spread_rows(a_ref, spread_ref)
    for m in range(KH):
        here = (KG % 8 + m) * (BS // 2)
        left = left_of(spread_ref[here : here + BS // 2, :])

        def table(s, m=m):
            return far[m][0, s * BS : (s + 1) * BS, :]

        put_right(right_ref, m, table)
        w = jnp.dot(left, right_ref[m], preferred_element_type=jnp.float32)
        for s in range(4):
            w_ref[m * 4 + s] = w[:, s * LANES : (s + 1) * LANES]

    def per_two(jj, carry):
        for t in range(2):
            j = jj * 2 + t
            here = i * KP + j
            add_matches(list_ref, here * FAR_E, count_ref[here], w_ref, m_ref.at[0, j])
        outs = []
        for t in range(2):
            j = jj * 2 + t
            for s in range(KC // 2):
                hi, lo = split(m_ref[0, j, s])
                cols = slice(s * LANES, (s + 1) * LANES)
                wide_ref[t, 0:64, cols] = hi
                wide_ref[t, 64:128, cols] = lo
                wide_ref[t, 128:192, cols] = hi
                wide_ref[t, 192:256, cols] = lo
            left = left_ref[0, pl.ds(pl.multiple_of(j * BS, BS), BS), :]
            outs.append(jnp.dot(left, wide_ref[t], preferred_element_type=jnp.float32))
        for t in range(2):
            pos = pos_ref[i * KP + jj * 2 + t]
            for s in range(KC // 2):
                acc_ref[pos, s * BS : (s + 1) * BS, :] += outs[t][:, s * LANES : (s + 1) * LANES]
        return carry

    lax.fori_loop(0, KP // 2, per_two, 0)

    @pl.when(i == pl.num_programs(0) - 1)
    def _():
        copies = [
            pltpu.make_async_copy(acc_ref.at[pl.ds(k * 8, out.shape[0])], out, sems.at[k])
            for k, out in enumerate((out0, out1, out2, out3, out4))
        ]
        for copy in copies:
            copy.start()
        for copy in copies:
            copy.wait()


def final_kernel(mine_ref, got_ref, out_ref, spread_ref):
    half = BS // 2
    first = first_half((half, LANES))
    for s in range(KC // 2):
        even, odd = (pl.ds(s * BS + o, half, stride=2) for o in range(2))
        even = mine_ref[0, even, :] + got_ref[0, even, :]
        odd = mine_ref[0, odd, :] + got_ref[0, odd, :]
        spread_ref[2 * s * half : (2 * s + 1) * half, :] = jnp.where(first, even, pltpu.roll(odd, BS, axis=1))
        spread_ref[(2 * s + 1) * half : (2 * s + 2) * half, :] = jnp.where(first, pltpu.roll(even, BS, axis=1), odd)
    for t in range(KC // 8):
        for k in range(half):
            out_ref[0, t * 8 : (t + 1) * 8, k * LANES : (k + 1) * LANES] = spread_ref[
                pl.ds(t * 8 * half + k, 8, stride=half), :
            ]


def outgoing_kernel(pick_ref, p_ref, out_ref, sem):
    n = out_ref.shape[0]

    def copy(k):
        src = p_ref.at[pl.ds(pl.multiple_of(pick_ref[k] * ROW_T, ROW_T), ROW_T)]
        return pltpu.make_async_copy(src, out_ref.at[k], sem.at[k])

    def start(k, carry):
        copy(k).start()
        return carry

    def wait(k, carry):
        copy(k).wait()
        return carry

    lax.fori_loop(0, n, start, 0)
    lax.fori_loop(0, n, wait, 0)


def match_lists(wanted, ids, live):
    n = ids.shape[1]
    eq = wanted[:, :, None] == ids[:, None, :]
    c_of = jnp.sum(jnp.where(eq, jnp.arange(KC, dtype=jnp.int32)[None, :, None], 0), axis=1)
    hit = jnp.any(eq, axis=1) & live
    number = jnp.arange(n, dtype=jnp.int32)
    before = jnp.sum(jnp.where((number[:, None] < number[None, :])[None], hit[:, :, None].astype(jnp.int32), 0), axis=1)
    code = number[None, :] * KC + c_of
    here = hit[:, None, :] & (before[:, None, :] == number[None, :, None])
    lists = jnp.sum(jnp.where(here, code[:, None, :], 0), axis=2)
    return lists.reshape(-1), jnp.sum(hit.astype(jnp.int32), axis=1)


def pick_rows(table, index):
    n = table.shape[0]
    one = index[:, None] == jnp.arange(n, dtype=jnp.int32)[None, :]
    return jnp.sum(jnp.where(one[:, :, None], table[None], 0), axis=1)


SIDE = 4


def places(device, me):
    x, y, k = device // (2 * SIDE), device // 2 % SIDE, device % 2
    return jnp.where(me % 2 == 0, x, y), jnp.where(me % 2 == 0, y, x), k


def device_at(u, v, k, me):
    u, v, k = u % SIDE, v % SIDE, k % 2
    return (jnp.where(me % 2 == 0, u, v) * SIDE + jnp.where(me % 2 == 0, v, u)) * 2 + k


def shift_pairs(shift, phase):
    pairs = []
    for x in range(SIDE):
        for y in range(SIDE):
            for k in range(2):
                along_x = (k == 0) == (phase == 0)
                to_x, to_y = ((x + shift) % SIDE, y) if along_x else (x, (y + shift) % SIDE)
                pairs.append(((x * SIDE + y) * 2 + k, (to_x * SIDE + to_y) * 2 + k))
    return pairs


def per_device(
    operator_blocks,
    operator_cols,
    halo_count,
    prolong_blocks,
    prolong_cols,
    prolong_slot,
    send_lists,
    slot_owner_row,
    coarse_pattern,
):
    n_dom = lax.axis_size("dom")
    n_grp = lax.axis_size("grp")
    g = lax.axis_index("grp")
    d = lax.axis_index("dom")
    owner = slot_owner_row.reshape(-1)

    panels = paired(prolong_blocks).reshape(RB * ROW_T, LANES)
    outgoing = pl.pallas_call(
        outgoing_kernel,
        out_shape=jax.ShapeDtypeStruct((n_dom, ROW_T, LANES), jnp.float32),
        grid_spec=pltpu.PrefetchScalarGridSpec(
            num_scalar_prefetch=1,
            grid=(1,),
            in_specs=[pl.BlockSpec((RB * ROW_T, LANES), lambda i, *_: (0, 0))],
            out_specs=pl.BlockSpec(memory_space=pltpu.HBM),
            scratch_shapes=[pltpu.SemaphoreType.DMA((n_dom,))],
        ),
        name="outgoing",
    )(send_lists.reshape(-1), panels)
    outgoing, panels, prolong_cols = lax.optimization_barrier((outgoing, panels, prolong_cols))
    far_rows = lax.all_to_all(outgoing, "dom", split_axis=0, concat_axis=0, tiled=True)

    id_tile = jnp.pad(prolong_cols.reshape(1, PAIRS).astype(jnp.float32), ((0, 7), (0, LANES - PAIRS)))
    carried = jnp.concatenate([panels, id_tile], axis=0)
    near_rows = [carried]
    for k in range(1, n_grp):
        near_rows.append(lax.ppermute(carried, "grp", [((z + k) % n_grp, z) for z in range(n_grp)]))

    mine = jnp.concatenate(
        [prolong_cols.reshape(-1), coarse_pattern.reshape(-1), send_lists.reshape(-1), owner.reshape(n_dom, 2)[:, 0]]
    )
    told = lax.all_to_all(
        jnp.broadcast_to(mine[None], (n_dom, mine.shape[0])), "dom", split_axis=0, concat_axis=0, tiled=True
    )
    all_cols = told[:, :PAIRS].reshape(n_dom, RB, KP)
    patterns = told[:, PAIRS : 2 * PAIRS].reshape(2 * n_dom, KC)
    here = jnp.arange(n_dom, dtype=jnp.int32)[None, :] == d
    picked = jnp.sum(jnp.where(here, told[:, 2 * PAIRS : 2 * PAIRS + n_dom], 0), axis=1)
    first_rows = told[:, 2 * PAIRS + n_dom :]
    far_ids = jnp.sum(
        jnp.where((picked[:, None] == jnp.arange(RB, dtype=jnp.int32))[:, :, None], all_cols, 0), axis=1
    )

    slots = prolong_slot.reshape(-1)
    slot_row = pick_rows(owner[:, None], slots)[:, 0]
    wanted = pick_rows(patterns, (slots // 2) * 2 + slot_row)
    u, v, k = places(d, d)
    to_u, to_v, to_k = places(slots // 2, d)
    position = ((to_u - u) % SIDE) * 8 + ((to_v - v) % SIDE) * 2 + (to_k - k) % 2
    position = jnp.where(slots % 2 == 1, n_dom, position)

    near_ids_table = jnp.concatenate(
        [rows[RB * ROW_T, :PAIRS].astype(jnp.int32).reshape(RB, KP) for rows in near_rows], axis=0
    )
    near_slots = operator_cols[:, :KG]
    near_cols = (((near_slots // RB) - g) % n_grp * RB + near_slots % RB).reshape(-1)
    far_cols = operator_cols[:, KG:].reshape(-1)
    near_ids = pick_rows(near_ids_table, near_cols).reshape(RB, NEAR_E)
    far_ids = pick_rows(far_ids, far_cols).reshape(RB, FAR_E)
    live = jnp.arange(KH, dtype=jnp.int32)[None, :] < halo_count[:, None]
    spread = lambda x: jnp.repeat(x, KP, axis=0)
    near_list, near_count = match_lists(wanted, spread(near_ids), jnp.ones((PAIRS, NEAR_E), bool))
    far_list, far_count = match_lists(wanted, spread(far_ids), spread(jnp.repeat(live, KP, axis=1)))

    row_block = pl.BlockSpec((RB * ROW_T, LANES), lambda i, *_: (0, 0))
    matched, left = pl.pallas_call(
        near_kernel,
        out_shape=(
            jax.ShapeDtypeStruct((RB, KP, KC // 2, BS, LANES), jnp.float32),
            jax.ShapeDtypeStruct((RB, KP * BS, 256), jnp.bfloat16),
        ),
        grid_spec=pltpu.PrefetchScalarGridSpec(
            num_scalar_prefetch=3,
            grid=(RB,),
            in_specs=[pl.BlockSpec((1, KA, BS * BS), lambda i, *_: (i, 0, 0))] + [row_block] * 4,
            out_specs=(
                pl.BlockSpec((1, KP, KC // 2, BS, LANES), lambda i, *_: (i, 0, 0, 0, 0)),
                pl.BlockSpec((1, KP * BS, 256), lambda i, *_: (i, 0, 0)),
            ),
            scratch_shapes=[
                pltpu.VMEM((4 * RB, 256, KP * BS), jnp.bfloat16),
                pltpu.VMEM((NEAR_E // 2, BS, LANES), jnp.float32),
                pltpu.VMEM((KA * BS // 2, LANES), jnp.float32),
            ],
        ),
        compiler_params=pltpu.CompilerParams(vmem_limit_bytes=40 * 2**20),
        cost_estimate=pl.CostEstimate(flops=10**10, bytes_accessed=16 * 2**20, transcendentals=0),
        name="near",
    )(near_cols, near_list, near_count, operator_blocks, *near_rows)

    far_spec = lambda m: pl.BlockSpec((1, ROW_T, LANES), lambda i, cols, *_: (cols[i * KH + m], 0, 0))
    slot_shape = (KC // 2 * BS, LANES)
    chunks = pl.pallas_call(
        far_kernel,
        out_shape=tuple(jax.ShapeDtypeStruct((n,) + slot_shape, jnp.float32) for n in (8, 8, 8, 8, 1)),
        grid_spec=pltpu.PrefetchScalarGridSpec(
            num_scalar_prefetch=4,
            grid=(RB,),
            in_specs=[pl.BlockSpec((1, 8, BS * BS), lambda i, *_: (i, 1, 0))]
            + [far_spec(m) for m in range(KH)]
            + [
                pl.BlockSpec((1, KP, KC // 2, BS, LANES), lambda i, *_: (i, 0, 0, 0, 0)),
                pl.BlockSpec((1, KP * BS, 256), lambda i, *_: (i, 0, 0)),
            ],
            out_specs=(pl.BlockSpec(memory_space=pltpu.HBM),) * 5,
            scratch_shapes=[
                pltpu.VMEM((KH, 256, KP * BS), jnp.bfloat16),
                pltpu.VMEM((FAR_E // 2, BS, LANES), jnp.float32),
                pltpu.VMEM((2, 256, KC * BS), jnp.bfloat16),
                pltpu.VMEM((n_dom + 1,) + slot_shape, jnp.float32),
                pltpu.VMEM((8 * BS // 2, LANES), jnp.float32),
                pltpu.SemaphoreType.DMA((5,)),
            ],
        ),
        compiler_params=pltpu.CompilerParams(vmem_limit_bytes=40 * 2**20),
        cost_estimate=pl.CostEstimate(flops=10**10, bytes_accessed=24 * 2**20, transcendentals=0),
        name="far",
    )(far_cols, far_list, far_count, position, operator_blocks, *([far_rows] * KH), matched, left)

    arriving = [chunks[0]] + [lax.ppermute(chunks[t], "dom", shift_pairs(t, 0)) for t in range(1, SIDE)]
    sources = jnp.stack([device_at(u - t, v, k, d) for t in range(SIDE)])
    owners = jnp.stack([device_at(u, v + p // 2, k + p % 2, d) for p in range(8)])
    rows_from = pick_rows(first_rows, sources)
    row_of = pick_rows(rows_from.T, owners).T
    own_first = row_of[0, 0]

    def owned(t2):
        total = 0.0
        for t in range(SIDE):
            part = arriving[t][2 * t2 : 2 * t2 + 2][:, None]
            to_row = row_of[t, 2 * t2 : 2 * t2 + 2][:, None] == jnp.arange(2, dtype=jnp.int32)
            total = total + jnp.where(to_row[:, :, None, None], part, 0.0)
        if t2 == 0:
            to_row = (jnp.arange(2, dtype=jnp.int32) == 1 - own_first)[None] & (jnp.arange(2) == 0)[:, None]
            total = total + jnp.where(to_row[:, :, None, None], chunks[4][:, None], 0.0)
        return total

    sent = {t2: lax.ppermute(owned(t2), "dom", shift_pairs(t2, 1)) for t2 in (2, 1, 3)}
    kept = owned(0)
    sums = [kept[kk] + sent[1][kk] + sent[2][kk] + sent[3][kk] for kk in (1, 0)]
    swapped = lax.ppermute(sums[0], "dom", [(n, n ^ 1) for n in range(n_dom)])

    row_spec = pl.BlockSpec((1,) + slot_shape, lambda i: (i, 0, 0))
    return pl.pallas_call(
        final_kernel,
        out_shape=jax.ShapeDtypeStruct((2, KC, BS * BS), jnp.float32),
        grid=(2,),
        in_specs=[row_spec, row_spec],
        out_specs=pl.BlockSpec((1, KC, BS * BS), lambda i: (i, 0, 0)),
        scratch_shapes=[pltpu.VMEM((KC * BS // 2, LANES), jnp.float32)],
        name="final",
    )(sums[1], swapped)


def solution(mesh):
    return jax.shard_map(
        per_device,
        mesh=mesh,
        in_specs=(
            P(("grp", "dom"), None, None),
            P(("grp", "dom"), None),
            P(("grp", "dom")),
            P(("grp", "dom"), None, None),
            P(("grp", "dom"), None),
            P(("grp", "dom"), None),
            P(("grp", "dom"), None),
            P(("grp", "dom"), None),
            P(("grp", "dom"), None),
        ),
        out_specs=P(("grp", "dom"), None, None),
        check_vma=False,
    )
```

```python
import functools

import jax
import jax.numpy as jnp
from jax import lax
from jax.experimental import pallas as pl
from jax.experimental.pallas import tpu as pltpu
from jax.sharding import PartitionSpec as P

BS = 64
KG = 12
KH = 4
KA = 16
KP = 8
KC = 16
RB = 4
PAIRS = RB * KP
NEAR_E = KG * KP
FAR_E = KH * KP
LANES = 128
STEP = 4
ROW_T = KP * BS * BS // LANES


def split(x):
    hi = x.astype(jnp.bfloat16)
    lo = (x - hi.astype(jnp.float32)).astype(jnp.bfloat16)
    return hi, lo


def paired(blocks):
    rows, n, _ = blocks.shape
    view = blocks.reshape(rows, n // 2, 2, BS, BS)
    return view.transpose(0, 1, 3, 2, 4).reshape(rows, n // 2, BS, LANES)


def first_half(shape):
    return lax.broadcasted_iota(jnp.int32, shape, 1) < BS


def put_right(right_ref, slot, table):
    for s in range(4):
        hi, lo = split(table(s))
        cols = slice(s * LANES, (s + 1) * LANES)
        right_ref[slot, 0:64, cols] = hi
        right_ref[slot, 64:128, cols] = hi
        right_ref[slot, 128:192, cols] = lo
        right_ref[slot, 192:256, cols] = lo


def spread_rows(a_ref, spread_ref):
    for t in range(a_ref.shape[1] // 8):
        for k in range(BS // 2):
            part = a_ref[0, t * 8 : (t + 1) * 8, k * LANES : (k + 1) * LANES]
            spread_ref[pl.ds(t * 8 * (BS // 2) + k, 8, stride=BS // 2), :] = part


def left_of(two):
    hi = two.astype(jnp.bfloat16).astype(jnp.float32)
    lo = pltpu.roll(two - hi, BS, axis=1)
    first = first_half(two.shape)
    rows = jnp.concatenate([jnp.where(first, hi, lo), jnp.where(first, lo, hi)], axis=0).astype(jnp.bfloat16)
    return jnp.concatenate([rows, rows], axis=1)


def put_weights(w_ref, m, w):
    for s in range(4):
        pair = w[:, s * LANES : (s + 1) * LANES]
        w_ref[0, m * 4 + s] = pair
        w_ref[1, m * 4 + s] = pltpu.roll(pair, BS, axis=1)


def add_matches(list_ref, base, count, w_ref, m_ref):
    half = lax.broadcasted_iota(jnp.int32, (BS, LANES), 1) // BS

    def body(k, carry):
        codes = [list_ref[base + k * STEP + t] for t in range(STEP)]
        parts = []
        for code in codes:
            e = code >> 4
            odd = code & 1
            parts.append(jnp.where(half == odd, w_ref[(e ^ code) & 1, e >> 1], 0.0))
        for code, part in zip(codes, parts):
            m_ref[(code & 15) >> 1] += part
        return carry

    lax.fori_loop(0, (count + STEP - 1) // STEP, body, 0)


def near_kernel(
    cols_ref, list_ref, count_ref, a_ref, p0, p1, p2, p3, m_ref, left_ref, right_ref, w_ref, spread_ref
):
    i = pl.program_id(0)

    @pl.when(i == 0)
    def _():
        for k, ref in enumerate((p0, p1, p2, p3)):

            def put(r, carry, k=k, ref=ref):
                def table(s):
                    return ref[pl.ds(pl.multiple_of(r * ROW_T + s * BS, BS), BS), :]

                put_right(right_ref, k * RB + r, table)
                return carry

            lax.fori_loop(0, RB, put, 0)

    for s in range(4):
        base = pl.multiple_of(i * ROW_T + s * BS, BS)
        slab = jnp.concatenate(
            [p0[pl.ds(base, BS // 2, stride=2), :], p0[pl.ds(base + 1, BS // 2, stride=2), :]], axis=0
        )
        hi = slab.astype(jnp.bfloat16).astype(jnp.float32)
        lo = slab - hi
        high = jnp.concatenate([hi, hi], axis=0).T.astype(jnp.bfloat16)
        low = jnp.concatenate([lo, lo], axis=0).T.astype(jnp.bfloat16)
        for t in range(2):
            left_ref[0, 2 * s + t, 0:BS, :] = high[t * BS : (t + 1) * BS]
            left_ref[0, 2 * s + t, BS : 2 * BS, :] = low[t * BS : (t + 1) * BS]

    for t in range(2):
        w_ref[t, NEAR_E // 2] = jnp.zeros((BS, LANES), jnp.float32)
    spread_rows(a_ref, spread_ref)
    for m in range(KG):
        left = left_of(spread_ref[m * (BS // 2) : (m + 1) * (BS // 2), :])
        w = jnp.dot(left, right_ref[cols_ref[i * KG + m]], preferred_element_type=jnp.float32)
        put_weights(w_ref, m, w)

    def per_target(j, carry):
        m_ref[0, j] = jnp.zeros((KC // 2, BS, LANES), jnp.float32)
        add_matches(list_ref, (i * KP + j) * NEAR_E, count_ref[i * KP + j], w_ref, m_ref.at[0, j])
        return carry

    lax.fori_loop(0, KP, per_target, 0)


def far_kernel(
    cols_ref, list_ref, count_ref, pos_ref, a_ref, f0, f1, f2, f3, m_ref, left_ref,
    out0, out1, out2, out3, out4, right_ref, w_ref, wide_ref, acc_ref, spread_ref, sems,
):
    i = pl.program_id(0)
    n_pos = acc_ref.shape[0]

    @pl.when(i == 0)
    def _():
        def clear(k, carry):
            acc_ref[k] = jnp.zeros(acc_ref.shape[1:], jnp.float32)
            return carry

        lax.fori_loop(0, n_pos, clear, 0)

    far = (f0, f1, f2, f3)
    for t in range(2):
        w_ref[t, FAR_E // 2] = jnp.zeros((BS, LANES), jnp.float32)
    spread_rows(a_ref, spread_ref)
    for m in range(KH):
        here = (KG % 8 + m) * (BS // 2)
        left = left_of(spread_ref[here : here + BS // 2, :])

        def table(s, m=m):
            return far[m][0, s * BS : (s + 1) * BS, :]

        put_right(right_ref, m, table)
        w = jnp.dot(left, right_ref[m], preferred_element_type=jnp.float32)
        put_weights(w_ref, m, w)

    def per_two(jj, carry):
        for t in range(2):
            j = jj * 2 + t
            here = i * KP + j
            add_matches(list_ref, here * FAR_E, count_ref[here], w_ref, m_ref.at[0, j])
        outs = []
        for t in range(2):
            j = jj * 2 + t
            for s in range(KC // 2):
                hi, lo = split(m_ref[0, j, s])
                cols = slice(s * LANES, (s + 1) * LANES)
                wide_ref[t, 0:64, cols] = hi
                wide_ref[t, 64:128, cols] = lo
            outs.append(jnp.dot(left_ref[0, j], wide_ref[t], preferred_element_type=jnp.float32))
        for t in range(2):
            pos = pos_ref[i * KP + jj * 2 + t]
            for s in range(KC // 2):
                cols = slice(s * LANES, (s + 1) * LANES)
                acc_ref[pos, s * BS : (s + 1) * BS, :] += outs[t][0:BS, cols] + outs[t][BS : 2 * BS, cols]
        return carry

    lax.fori_loop(0, KP // 2, per_two, 0)

    @pl.when(i == pl.num_programs(0) - 1)
    def _():
        copies = [
            pltpu.make_async_copy(acc_ref.at[pl.ds(k * 8, out.shape[0])], out, sems.at[k])
            for k, out in enumerate((out0, out1, out2, out3, out4))
        ]
        for copy in copies:
            copy.start()
        for copy in copies:
            copy.wait()


def final_kernel(mine_ref, got_ref, out_ref, spread_ref):
    half = BS // 2
    first = first_half((half, LANES))
    for s in range(KC // 2):
        even, odd = (pl.ds(s * BS + o, half, stride=2) for o in range(2))
        even = mine_ref[0, even, :] + got_ref[0, even, :]
        odd = mine_ref[0, odd, :] + got_ref[0, odd, :]
        spread_ref[2 * s * half : (2 * s + 1) * half, :] = jnp.where(first, even, pltpu.roll(odd, BS, axis=1))
        spread_ref[(2 * s + 1) * half : (2 * s + 2) * half, :] = jnp.where(first, pltpu.roll(even, BS, axis=1), odd)
    for t in range(KC // 8):
        for k in range(half):
            out_ref[0, t * 8 : (t + 1) * 8, k * LANES : (k + 1) * LANES] = spread_ref[
                pl.ds(t * 8 * half + k, 8, stride=half), :
            ]


def outgoing_kernel(pick_ref, p_ref, out_ref, sem):
    n = out_ref.shape[0]

    def copy(k):
        src = p_ref.at[pl.ds(pl.multiple_of(pick_ref[k] * ROW_T, ROW_T), ROW_T)]
        return pltpu.make_async_copy(src, out_ref.at[k], sem.at[k])

    def start(k, carry):
        copy(k).start()
        return carry

    def wait(k, carry):
        copy(k).wait()
        return carry

    lax.fori_loop(0, n, start, 0)
    lax.fori_loop(0, n, wait, 0)


def match_lists(wanted, ids, live):
    n = ids.shape[1]
    eq = wanted[:, :, None] == ids[:, None, :]
    c_of = jnp.sum(jnp.where(eq, jnp.arange(KC, dtype=jnp.int32)[None, :, None], 0), axis=1)
    hit = jnp.any(eq, axis=1) & live
    number = jnp.arange(n, dtype=jnp.int32)
    before = jnp.sum(jnp.where((number[:, None] < number[None, :])[None], hit[:, :, None].astype(jnp.int32), 0), axis=1)
    code = number[None, :] * KC + c_of
    here = hit[:, None, :] & (before[:, None, :] == number[None, :, None])
    count = jnp.sum(hit.astype(jnp.int32), axis=1)
    lists = jnp.sum(jnp.where(here, code[:, None, :], 0), axis=2)
    lists = jnp.where(number[None, :] < count[:, None], lists, n * KC)
    return lists.reshape(-1), count


def pick_rows(table, index):
    n = table.shape[0]
    one = index[:, None] == jnp.arange(n, dtype=jnp.int32)[None, :]
    return jnp.sum(jnp.where(one[:, :, None], table[None], 0), axis=1)


def near_call(cols, lists, counts, operator_blocks, near_rows):
    row_block = pl.BlockSpec((RB * ROW_T, LANES), lambda i, *_: (0, 0))
    return pl.pallas_call(
        near_kernel,
        out_shape=(
            jax.ShapeDtypeStruct((RB, KP, KC // 2, BS, LANES), jnp.float32),
            jax.ShapeDtypeStruct((RB, KP, LANES, LANES), jnp.bfloat16),
        ),
        grid_spec=pltpu.PrefetchScalarGridSpec(
            num_scalar_prefetch=3,
            grid=(RB,),
            in_specs=[pl.BlockSpec((1, KA, BS * BS), lambda i, *_: (i, 0, 0))] + [row_block] * 4,
            out_specs=(
                pl.BlockSpec((1, KP, KC // 2, BS, LANES), lambda i, *_: (i, 0, 0, 0, 0)),
                pl.BlockSpec((1, KP, LANES, LANES), lambda i, *_: (i, 0, 0, 0)),
            ),
            scratch_shapes=[
                pltpu.VMEM((4 * RB, 256, KP * BS), jnp.bfloat16),
                pltpu.VMEM((2, NEAR_E // 2 + 1, BS, LANES), jnp.float32),
                pltpu.VMEM((KA * BS // 2, LANES), jnp.float32),
            ],
        ),
        compiler_params=pltpu.CompilerParams(vmem_limit_bytes=40 * 2**20),
        cost_estimate=pl.CostEstimate(flops=10**10, bytes_accessed=16 * 2**20, transcendentals=0),
        name="near",
    )(cols, lists, counts, operator_blocks, *near_rows)


def far_call(cols, lists, counts, position, operator_blocks, far_rows, matched, left, n_dom):
    far_spec = lambda m: pl.BlockSpec((1, ROW_T, LANES), lambda i, cols, *_: (cols[i * KH + m], 0, 0))
    slot_shape = (KC // 2 * BS, LANES)
    return pl.pallas_call(
        far_kernel,
        out_shape=tuple(jax.ShapeDtypeStruct((n,) + slot_shape, jnp.float32) for n in (8, 8, 8, 8, 1)),
        grid_spec=pltpu.PrefetchScalarGridSpec(
            num_scalar_prefetch=4,
            grid=(RB,),
            in_specs=[pl.BlockSpec((1, 8, BS * BS), lambda i, *_: (i, 1, 0))]
            + [far_spec(m) for m in range(KH)]
            + [
                pl.BlockSpec((1, KP, KC // 2, BS, LANES), lambda i, *_: (i, 0, 0, 0, 0)),
                pl.BlockSpec((1, KP, LANES, LANES), lambda i, *_: (i, 0, 0, 0)),
            ],
            out_specs=(pl.BlockSpec(memory_space=pltpu.HBM),) * 5,
            scratch_shapes=[
                pltpu.VMEM((KH, 256, KP * BS), jnp.bfloat16),
                pltpu.VMEM((2, FAR_E // 2 + 1, BS, LANES), jnp.float32),
                pltpu.VMEM((2, LANES, KC * BS), jnp.bfloat16),
                pltpu.VMEM((n_dom + 1,) + slot_shape, jnp.float32),
                pltpu.VMEM((8 * BS // 2, LANES), jnp.float32),
                pltpu.SemaphoreType.DMA((5,)),
            ],
        ),
        compiler_params=pltpu.CompilerParams(vmem_limit_bytes=40 * 2**20),
        cost_estimate=pl.CostEstimate(flops=10**10, bytes_accessed=24 * 2**20, transcendentals=0),
        name="far",
    )(cols, lists, counts, position, operator_blocks, *([far_rows] * KH), matched, left)


SIDE = 4


def places(device, me):
    x, y, k = device // (2 * SIDE), device // 2 % SIDE, device % 2
    return jnp.where(me % 2 == 0, x, y), jnp.where(me % 2 == 0, y, x), k


def device_at(u, v, k, me):
    u, v, k = u % SIDE, v % SIDE, k % 2
    return (jnp.where(me % 2 == 0, u, v) * SIDE + jnp.where(me % 2 == 0, v, u)) * 2 + k


def shift_pairs(shift, phase):
    pairs = []
    for x in range(SIDE):
        for y in range(SIDE):
            for k in range(2):
                along_x = (k == 0) == (phase == 0)
                to_x, to_y = ((x + shift) % SIDE, y) if along_x else (x, (y + shift) % SIDE)
                pairs.append(((x * SIDE + y) * 2 + k, (to_x * SIDE + to_y) * 2 + k))
    return pairs


def per_device(
    operator_blocks,
    operator_cols,
    halo_count,
    prolong_blocks,
    prolong_cols,
    prolong_slot,
    send_lists,
    slot_owner_row,
    coarse_pattern,
):
    n_dom = lax.axis_size("dom")
    n_grp = lax.axis_size("grp")
    g = lax.axis_index("grp")
    d = lax.axis_index("dom")
    owner = slot_owner_row.reshape(-1)

    panels = paired(prolong_blocks).reshape(RB * ROW_T, LANES)
    outgoing = pl.pallas_call(
        outgoing_kernel,
        out_shape=jax.ShapeDtypeStruct((n_dom, ROW_T, LANES), jnp.float32),
        grid_spec=pltpu.PrefetchScalarGridSpec(
            num_scalar_prefetch=1,
            grid=(1,),
            in_specs=[pl.BlockSpec((RB * ROW_T, LANES), lambda i, *_: (0, 0))],
            out_specs=pl.BlockSpec(memory_space=pltpu.HBM),
            scratch_shapes=[pltpu.SemaphoreType.DMA((n_dom,))],
        ),
        name="outgoing",
    )(send_lists.reshape(-1), panels)
    far_rows = lax.all_to_all(outgoing, "dom", split_axis=0, concat_axis=0, tiled=True)

    id_tile = jnp.pad(prolong_cols.reshape(1, PAIRS).astype(jnp.float32), ((0, 7), (0, LANES - PAIRS)))
    carried = jnp.concatenate([panels, id_tile], axis=0)
    near_rows = [carried]
    for k in range(1, n_grp):
        near_rows.append(lax.ppermute(carried, "grp", [((z + k) % n_grp, z) for z in range(n_grp)]))

    mine = jnp.concatenate(
        [prolong_cols.reshape(-1), coarse_pattern.reshape(-1), send_lists.reshape(-1), owner.reshape(n_dom, 2)[:, 0]]
    )
    told = lax.all_to_all(
        jnp.broadcast_to(mine[None], (n_dom, mine.shape[0])), "dom", split_axis=0, concat_axis=0, tiled=True
    )
    all_cols = told[:, :PAIRS].reshape(n_dom, RB, KP)
    patterns = told[:, PAIRS : 2 * PAIRS].reshape(2 * n_dom, KC)
    here = jnp.arange(n_dom, dtype=jnp.int32)[None, :] == d
    picked = jnp.sum(jnp.where(here, told[:, 2 * PAIRS : 2 * PAIRS + n_dom], 0), axis=1)
    first_rows = told[:, 2 * PAIRS + n_dom :]
    far_ids = jnp.sum(
        jnp.where((picked[:, None] == jnp.arange(RB, dtype=jnp.int32))[:, :, None], all_cols, 0), axis=1
    )

    slots = prolong_slot.reshape(-1)
    slot_row = pick_rows(owner[:, None], slots)[:, 0]
    wanted = pick_rows(patterns, (slots // 2) * 2 + slot_row)
    u, v, k = places(d, d)
    to_u, to_v, to_k = places(slots // 2, d)
    position = ((to_u - u) % SIDE) * 8 + ((to_v - v) % SIDE) * 2 + (to_k - k) % 2
    position = jnp.where(slots % 2 == 1, n_dom, position)

    near_ids_table = jnp.concatenate(
        [rows[RB * ROW_T, :PAIRS].astype(jnp.int32).reshape(RB, KP) for rows in near_rows], axis=0
    )
    near_slots = operator_cols[:, :KG]
    near_cols = (((near_slots // RB) - g) % n_grp * RB + near_slots % RB).reshape(-1)
    far_cols = operator_cols[:, KG:].reshape(-1)
    near_ids = pick_rows(near_ids_table, near_cols).reshape(RB, NEAR_E)
    far_ids = pick_rows(far_ids, far_cols).reshape(RB, FAR_E)
    live = jnp.arange(KH, dtype=jnp.int32)[None, :] < halo_count[:, None]
    spread = lambda x: jnp.repeat(x, KP, axis=0)
    near_list, near_count = match_lists(wanted, spread(near_ids), jnp.ones((PAIRS, NEAR_E), bool))
    far_list, far_count = match_lists(wanted, spread(far_ids), spread(jnp.repeat(live, KP, axis=1)))

    matched, left = near_call(near_cols, near_list, near_count, operator_blocks, near_rows)
    chunks = far_call(far_cols, far_list, far_count, position, operator_blocks, far_rows, matched, left, n_dom)
    slot_shape = (KC // 2 * BS, LANES)

    arriving = [chunks[0]] + [lax.ppermute(chunks[t], "dom", shift_pairs(t, 0)) for t in range(1, SIDE)]
    sources = jnp.stack([device_at(u - t, v, k, d) for t in range(SIDE)])
    owners = jnp.stack([device_at(u, v + p // 2, k + p % 2, d) for p in range(8)])
    rows_from = pick_rows(first_rows, sources)
    row_of = pick_rows(rows_from.T, owners).T
    own_first = row_of[0, 0]

    def owned(t2):
        total = 0.0
        for t in range(SIDE):
            part = arriving[t][2 * t2 : 2 * t2 + 2][:, None]
            to_row = row_of[t, 2 * t2 : 2 * t2 + 2][:, None] == jnp.arange(2, dtype=jnp.int32)
            total = total + jnp.where(to_row[:, :, None, None], part, 0.0)
        if t2 == 0:
            to_row = (jnp.arange(2, dtype=jnp.int32) == 1 - own_first)[None] & (jnp.arange(2) == 0)[:, None]
            total = total + jnp.where(to_row[:, :, None, None], chunks[4][:, None], 0.0)
        return total

    sent = {t2: lax.ppermute(owned(t2), "dom", shift_pairs(t2, 1)) for t2 in (2, 1, 3)}
    kept = owned(0)
    sums = [kept[kk] + sent[1][kk] + sent[2][kk] + sent[3][kk] for kk in (1, 0)]
    swapped = lax.ppermute(sums[0], "dom", [(n, n ^ 1) for n in range(n_dom)])

    row_spec = pl.BlockSpec((1,) + slot_shape, lambda i: (i, 0, 0))
    return pl.pallas_call(
        final_kernel,
        out_shape=jax.ShapeDtypeStruct((2, KC, BS * BS), jnp.float32),
        grid=(2,),
        in_specs=[row_spec, row_spec],
        out_specs=pl.BlockSpec((1, KC, BS * BS), lambda i: (i, 0, 0)),
        scratch_shapes=[pltpu.VMEM((KC * BS // 2, LANES), jnp.float32)],
        name="final",
    )(sums[1], swapped)


def solution(mesh):
    return jax.shard_map(
        per_device,
        mesh=mesh,
        in_specs=(
            P(("grp", "dom"), None, None),
            P(("grp", "dom"), None),
            P(("grp", "dom")),
            P(("grp", "dom"), None, None),
            P(("grp", "dom"), None),
            P(("grp", "dom"), None),
            P(("grp", "dom"), None),
            P(("grp", "dom"), None),
            P(("grp", "dom"), None),
        ),
        out_specs=P(("grp", "dom"), None, None),
        check_vma=False,
    )
```

```python
import functools

import jax
import jax.numpy as jnp
from jax import lax
from jax.experimental import pallas as pl
from jax.experimental.pallas import tpu as pltpu
from jax.sharding import PartitionSpec as P

BS = 64
KG = 12
KH = 4
KA = 16
KP = 8
KC = 16
HALVES = 2
OUT_SPACE = pl.ANY
FAR_VMEM = 24
HALF_C = KC // HALVES
RB = 4
PAIRS = RB * KP
NEAR_E = KG * KP
FAR_E = KH * KP
LANES = 128
STEP = 4
ROW_T = KP * BS * BS // LANES


def split(x):
    hi = x.astype(jnp.bfloat16)
    lo = (x - hi.astype(jnp.float32)).astype(jnp.bfloat16)
    return hi, lo


def paired(blocks):
    rows, n, _ = blocks.shape
    view = blocks.reshape(rows, n // 2, 2, BS, BS)
    return view.transpose(0, 1, 3, 2, 4).reshape(rows, n // 2, BS, LANES)


def first_half(shape):
    return lax.broadcasted_iota(jnp.int32, shape, 1) < BS


def put_right(right_ref, slot, table):
    for s in range(4):
        hi, lo = split(table(s))
        cols = slice(s * LANES, (s + 1) * LANES)
        right_ref[slot, 0:64, cols] = hi
        right_ref[slot, 64:128, cols] = hi
        right_ref[slot, 128:192, cols] = lo
        right_ref[slot, 192:256, cols] = lo


def spread_rows(a_ref, spread_ref):
    for t in range(a_ref.shape[1] // 8):
        for k in range(BS // 2):
            part = a_ref[0, t * 8 : (t + 1) * 8, k * LANES : (k + 1) * LANES]
            spread_ref[pl.ds(t * 8 * (BS // 2) + k, 8, stride=BS // 2), :] = part


def left_of(two):
    hi = two.astype(jnp.bfloat16).astype(jnp.float32)
    lo = pltpu.roll(two - hi, BS, axis=1)
    first = first_half(two.shape)
    rows = jnp.concatenate([jnp.where(first, hi, lo), jnp.where(first, lo, hi)], axis=0).astype(jnp.bfloat16)
    return jnp.concatenate([rows, rows], axis=1)


def put_weights(w_ref, m, w):
    for s in range(4):
        pair = w[:, s * LANES : (s + 1) * LANES]
        w_ref[0, m * 4 + s] = pair
        w_ref[1, m * 4 + s] = pltpu.roll(pair, BS, axis=1)


def add_matches(list_ref, base, count, w_ref, m_ref):
    half = lax.broadcasted_iota(jnp.int32, (BS, LANES), 1) // BS

    def body(k, carry):
        codes = [list_ref[base + k * STEP + t] for t in range(STEP)]
        parts = []
        for code in codes:
            e = code >> 4
            odd = code & 1
            parts.append(jnp.where(half == odd, w_ref[(e ^ code) & 1, e >> 1], 0.0))
        for code, part in zip(codes, parts):
            m_ref[(code & 15) >> 1] += part
        return carry

    lax.fori_loop(0, (count + STEP - 1) // STEP, body, 0)


def near_kernel(
    cols_ref, list_ref, count_ref, a_ref, p0, p1, p2, p3, m_ref, left_ref, right_ref, w_ref, spread_ref
):
    i = pl.program_id(0)

    @pl.when(i == 0)
    def _():
        for k, ref in enumerate((p0, p1, p2, p3)):

            def put(r, carry, k=k, ref=ref):
                def table(s):
                    return ref[pl.ds(pl.multiple_of(r * ROW_T + s * BS, BS), BS), :]

                put_right(right_ref, k * RB + r, table)
                return carry

            lax.fori_loop(0, RB, put, 0)

    for s in range(4):
        base = pl.multiple_of(i * ROW_T + s * BS, BS)
        slab = jnp.concatenate(
            [p0[pl.ds(base, BS // 2, stride=2), :], p0[pl.ds(base + 1, BS // 2, stride=2), :]], axis=0
        )
        hi = slab.astype(jnp.bfloat16).astype(jnp.float32)
        lo = slab - hi
        high = jnp.concatenate([hi, hi], axis=0).T.astype(jnp.bfloat16)
        low = jnp.concatenate([lo, lo], axis=0).T.astype(jnp.bfloat16)
        for t in range(2):
            left_ref[0, 2 * s + t, 0:BS, :] = high[t * BS : (t + 1) * BS]
            left_ref[0, 2 * s + t, BS : 2 * BS, :] = low[t * BS : (t + 1) * BS]

    for t in range(2):
        w_ref[t, NEAR_E // 2] = jnp.zeros((BS, LANES), jnp.float32)
    spread_rows(a_ref, spread_ref)
    for m in range(KG):
        left = left_of(spread_ref[m * (BS // 2) : (m + 1) * (BS // 2), :])
        w = jnp.dot(left, right_ref[cols_ref[i * KG + m]], preferred_element_type=jnp.float32)
        put_weights(w_ref, m, w)

    def per_target(j, carry):
        m_ref[0, j] = jnp.zeros((KC // 2, BS, LANES), jnp.float32)
        add_matches(list_ref, (i * KP + j) * NEAR_E, count_ref[i * KP + j], w_ref, m_ref.at[0, j])
        return carry

    lax.fori_loop(0, KP, per_target, 0)


def far_kernel(
    cols_ref, list_ref, count_ref, pos_ref, a_ref, f0, f1, f2, f3, m_ref, left_ref,
    out0, out1, out2, out3, out4, right_ref, w_ref, wide_ref, acc_ref, spread_ref, sems,
):
    i = pl.program_id(0)
    n_pos = acc_ref.shape[0]

    @pl.when(i == 0)
    def _():
        def clear(k, carry):
            acc_ref[k] = jnp.zeros(acc_ref.shape[1:], jnp.float32)
            return carry

        lax.fori_loop(0, n_pos, clear, 0)

    far = (f0, f1, f2, f3)
    for t in range(2):
        w_ref[t, FAR_E // 2] = jnp.zeros((BS, LANES), jnp.float32)
    spread_rows(a_ref, spread_ref)
    for m in range(KH):
        here = (KG % 8 + m) * (BS // 2)
        left = left_of(spread_ref[here : here + BS // 2, :])

        def table(s, m=m):
            return far[m][0, s * BS : (s + 1) * BS, :]

        put_right(right_ref, m, table)
        w = jnp.dot(left, right_ref[m], preferred_element_type=jnp.float32)
        put_weights(w_ref, m, w)

    def per_two(jj, carry):
        for t in range(2):
            j = jj * 2 + t
            here = i * KP + j
            add_matches(list_ref, here * FAR_E, count_ref[here], w_ref, m_ref.at[0, j])
        outs = []
        for t in range(2):
            j = jj * 2 + t
            for s in range(HALF_C // 2):
                hi, lo = split(m_ref[0, j, s])
                cols = slice(s * LANES, (s + 1) * LANES)
                wide_ref[t, 0:64, cols] = hi
                wide_ref[t, 64:128, cols] = lo
            outs.append(jnp.dot(left_ref[0, j], wide_ref[t], preferred_element_type=jnp.float32))
        for t in range(2):
            pos = pos_ref[i * KP + jj * 2 + t]
            for s in range(HALF_C // 2):
                cols = slice(s * LANES, (s + 1) * LANES)
                acc_ref[pos, s * BS : (s + 1) * BS, :] += outs[t][0:BS, cols] + outs[t][BS : 2 * BS, cols]
        return carry

    lax.fori_loop(0, KP // 2, per_two, 0)

    @pl.when(i == pl.num_programs(0) - 1)
    def _():
        copies = [
            pltpu.make_async_copy(acc_ref.at[pl.ds(k * 8, out.shape[0])], out, sems.at[k])
            for k, out in enumerate((out0, out1, out2, out3, out4))
        ]
        for copy in copies:
            copy.start()
        for copy in copies:
            copy.wait()


def final_kernel(*refs):
    *parts, out_ref, spread_ref = refs
    half = BS // 2
    first = first_half((half, LANES))
    for s in range(KC // 2):
        mine_ref, got_ref = parts[2 * (s // (HALF_C // 2)) : 2 * (s // (HALF_C // 2)) + 2]
        even, odd = (pl.ds(s % (HALF_C // 2) * BS + o, half, stride=2) for o in range(2))
        even = mine_ref[0, even, :] + got_ref[0, even, :]
        odd = mine_ref[0, odd, :] + got_ref[0, odd, :]
        spread_ref[2 * s * half : (2 * s + 1) * half, :] = jnp.where(first, even, pltpu.roll(odd, BS, axis=1))
        spread_ref[(2 * s + 1) * half : (2 * s + 2) * half, :] = jnp.where(first, pltpu.roll(even, BS, axis=1), odd)
    for t in range(KC // 8):
        for k in range(half):
            out_ref[0, t * 8 : (t + 1) * 8, k * LANES : (k + 1) * LANES] = spread_ref[
                pl.ds(t * 8 * half + k, 8, stride=half), :
            ]


def outgoing_kernel(pick_ref, p_ref, out_ref, sem):
    n = out_ref.shape[0]

    def copy(k):
        src = p_ref.at[pl.ds(pl.multiple_of(pick_ref[k] * ROW_T, ROW_T), ROW_T)]
        return pltpu.make_async_copy(src, out_ref.at[k], sem.at[k])

    def start(k, carry):
        copy(k).start()
        return carry

    def wait(k, carry):
        copy(k).wait()
        return carry

    lax.fori_loop(0, n, start, 0)
    lax.fori_loop(0, n, wait, 0)


def match_lists(wanted, ids, live):
    n = ids.shape[1]
    eq = wanted[:, :, None] == ids[:, None, :]
    c_of = jnp.sum(jnp.where(eq, jnp.arange(wanted.shape[1], dtype=jnp.int32)[None, :, None], 0), axis=1)
    hit = jnp.any(eq, axis=1) & live
    number = jnp.arange(n, dtype=jnp.int32)
    before = jnp.sum(jnp.where((number[:, None] < number[None, :])[None], hit[:, :, None].astype(jnp.int32), 0), axis=1)
    code = number[None, :] * KC + c_of
    here = hit[:, None, :] & (before[:, None, :] == number[None, :, None])
    count = jnp.sum(hit.astype(jnp.int32), axis=1)
    lists = jnp.sum(jnp.where(here, code[:, None, :], 0), axis=2)
    lists = jnp.where(number[None, :] < count[:, None], lists, n * KC)
    return lists.reshape(-1), count


def pick_rows(table, index):
    n = table.shape[0]
    one = index[:, None] == jnp.arange(n, dtype=jnp.int32)[None, :]
    return jnp.sum(jnp.where(one[:, :, None], table[None], 0), axis=1)


def near_call(cols, lists, counts, operator_blocks, near_rows):
    row_block = pl.BlockSpec((RB * ROW_T, LANES), lambda i, *_: (0, 0))
    return pl.pallas_call(
        near_kernel,
        out_shape=(
            jax.ShapeDtypeStruct((RB, KP, KC // 2, BS, LANES), jnp.float32),
            jax.ShapeDtypeStruct((RB, KP, LANES, LANES), jnp.bfloat16),
        ),
        grid_spec=pltpu.PrefetchScalarGridSpec(
            num_scalar_prefetch=3,
            grid=(RB,),
            in_specs=[pl.BlockSpec((1, KA, BS * BS), lambda i, *_: (i, 0, 0))] + [row_block] * 4,
            out_specs=(
                pl.BlockSpec((1, KP, KC // 2, BS, LANES), lambda i, *_: (i, 0, 0, 0, 0)),
                pl.BlockSpec((1, KP, LANES, LANES), lambda i, *_: (i, 0, 0, 0)),
            ),
            scratch_shapes=[
                pltpu.VMEM((4 * RB, 256, KP * BS), jnp.bfloat16),
                pltpu.VMEM((2, NEAR_E // 2 + 1, BS, LANES), jnp.float32),
                pltpu.VMEM((KA * BS // 2, LANES), jnp.float32),
            ],
        ),
        compiler_params=pltpu.CompilerParams(vmem_limit_bytes=40 * 2**20),
        cost_estimate=pl.CostEstimate(flops=10**10, bytes_accessed=16 * 2**20, transcendentals=0),
        name="near",
    )(cols, lists, counts, operator_blocks, *near_rows)


def far_call(half, cols, lists, counts, position, operator_blocks, far_rows, matched, left, n_dom):
    far_spec = lambda m: pl.BlockSpec((1, ROW_T, LANES), lambda i, cols, *_: (cols[i * KH + m], 0, 0))
    slot_shape = (HALF_C // 2 * BS, LANES)
    hbm = lambda x: pltpu.with_memory_space_constraint(x, pltpu.HBM)
    return pl.pallas_call(
        far_kernel,
        out_shape=tuple(jax.ShapeDtypeStruct((n,) + slot_shape, jnp.float32) for n in (8, 8, 8, 8, 1)),
        grid_spec=pltpu.PrefetchScalarGridSpec(
            num_scalar_prefetch=4,
            grid=(RB,),
            in_specs=[pl.BlockSpec((1, 8, BS * BS), lambda i, *_: (i, 1, 0))]
            + [far_spec(m) for m in range(KH)]
            + [
                pl.BlockSpec((1, KP, HALF_C // 2, BS, LANES), lambda i, *_: (i, 0, half, 0, 0)),
                pl.BlockSpec((1, KP, LANES, LANES), lambda i, *_: (i, 0, 0, 0)),
            ],
            out_specs=(pl.BlockSpec(memory_space=OUT_SPACE),) * 5,
            scratch_shapes=[
                pltpu.VMEM((KH, 256, KP * BS), jnp.bfloat16),
                pltpu.VMEM((2, FAR_E // 2 + 1, BS, LANES), jnp.float32),
                pltpu.VMEM((2, LANES, HALF_C * BS), jnp.bfloat16),
                pltpu.VMEM((n_dom + 1,) + slot_shape, jnp.float32),
                pltpu.VMEM((8 * BS // 2, LANES), jnp.float32),
                pltpu.SemaphoreType.DMA((5,)),
            ],
        ),
        compiler_params=pltpu.CompilerParams(vmem_limit_bytes=FAR_VMEM * 2**20),
        cost_estimate=pl.CostEstimate(flops=5 * 10**9, bytes_accessed=12 * 2**20, transcendentals=0),
        name="far",
    )(cols, lists, counts, position, operator_blocks, *([far_rows] * KH), hbm(matched), hbm(left))


SIDE = 4


def places(device, me):
    x, y, k = device // (2 * SIDE), device // 2 % SIDE, device % 2
    return jnp.where(me % 2 == 0, x, y), jnp.where(me % 2 == 0, y, x), k


def device_at(u, v, k, me):
    u, v, k = u % SIDE, v % SIDE, k % 2
    return (jnp.where(me % 2 == 0, u, v) * SIDE + jnp.where(me % 2 == 0, v, u)) * 2 + k


def plane_pairs(dx, dy, dk):
    return [
        ((((x + dx) % SIDE) * SIDE + (y + dy) % SIDE) * 2 + (k + dk) % 2, (x * SIDE + y) * 2 + k)
        for x in range(SIDE)
        for y in range(SIDE)
        for k in range(2)
    ]


def shift_pairs(shift, phase):
    pairs = []
    for x in range(SIDE):
        for y in range(SIDE):
            for k in range(2):
                along_x = (k == 0) == (phase == 0)
                to_x, to_y = ((x + shift) % SIDE, y) if along_x else (x, (y + shift) % SIDE)
                pairs.append(((x * SIDE + y) * 2 + k, (to_x * SIDE + to_y) * 2 + k))
    return pairs


def per_device(
    operator_blocks,
    operator_cols,
    halo_count,
    prolong_blocks,
    prolong_cols,
    prolong_slot,
    send_lists,
    slot_owner_row,
    coarse_pattern,
):
    n_dom = lax.axis_size("dom")
    n_grp = lax.axis_size("grp")
    g = lax.axis_index("grp")
    d = lax.axis_index("dom")
    owner = slot_owner_row.reshape(-1)

    panels = paired(prolong_blocks).reshape(RB * ROW_T, LANES)
    outgoing = pl.pallas_call(
        outgoing_kernel,
        out_shape=jax.ShapeDtypeStruct((n_dom, ROW_T, LANES), jnp.float32),
        grid_spec=pltpu.PrefetchScalarGridSpec(
            num_scalar_prefetch=1,
            grid=(1,),
            in_specs=[pl.BlockSpec((RB * ROW_T, LANES), lambda i, *_: (0, 0))],
            out_specs=pl.BlockSpec(memory_space=pltpu.HBM),
            scratch_shapes=[pltpu.SemaphoreType.DMA((n_dom,))],
        ),
        name="outgoing",
    )(send_lists.reshape(-1), panels)
    outgoing, prolong_cols, panels = lax.optimization_barrier((outgoing, prolong_cols, panels))
    far_rows = lax.all_to_all(outgoing, "dom", split_axis=0, concat_axis=0, tiled=True)

    id_tile = jnp.pad(prolong_cols.reshape(1, PAIRS).astype(jnp.float32), ((0, 7), (0, LANES - PAIRS)))
    carried = jnp.concatenate([panels, id_tile], axis=0)
    near_rows = [carried]
    for k in range(1, n_grp):
        near_rows.append(lax.ppermute(carried, "grp", [((z + k) % n_grp, z) for z in range(n_grp)]))

    mine = jnp.concatenate(
        [prolong_cols.reshape(-1), coarse_pattern.reshape(-1), send_lists.reshape(-1), owner.reshape(n_dom, 2)[:, 0]]
    )
    told = mine[None]
    told = jnp.concatenate([told, lax.ppermute(told, "dom", plane_pairs(0, 0, 1))], axis=0)
    told = jnp.concatenate([told] + [lax.ppermute(told, "dom", plane_pairs(0, n, 0)) for n in range(1, SIDE)], axis=0)
    told = jnp.concatenate([told] + [lax.ppermute(told, "dom", plane_pairs(n, 0, 0)) for n in range(1, SIDE)], axis=0)

    def relative(device):
        dx = device // (2 * SIDE) - d // (2 * SIDE)
        dy = device // 2 % SIDE - d // 2 % SIDE
        return ((dx % SIDE) * SIDE + dy % SIDE) * 2 + (device - d) % 2

    all_cols = told[:, :PAIRS].reshape(n_dom, RB, KP)
    patterns = told[:, PAIRS : 2 * PAIRS].reshape(2 * n_dom, KC)
    here = jnp.arange(n_dom, dtype=jnp.int32)[None, :] == d
    picked = jnp.sum(jnp.where(here, told[:, 2 * PAIRS : 2 * PAIRS + n_dom], 0), axis=1)
    first_rows = told[:, 2 * PAIRS + n_dom :]
    far_ids = jnp.sum(
        jnp.where((picked[:, None] == jnp.arange(RB, dtype=jnp.int32))[:, :, None], all_cols, 0), axis=1
    )

    slots = prolong_slot.reshape(-1)
    slot_row = pick_rows(owner[:, None], slots)[:, 0]
    wanted = pick_rows(patterns, relative(slots // 2) * 2 + slot_row)
    u, v, k = places(d, d)
    to_u, to_v, to_k = places(slots // 2, d)
    position = ((to_u - u) % SIDE) * 8 + ((to_v - v) % SIDE) * 2 + (to_k - k) % 2
    position = jnp.where(slots % 2 == 1, n_dom, position)

    near_ids_table = jnp.concatenate(
        [rows[RB * ROW_T, :PAIRS].astype(jnp.int32).reshape(RB, KP) for rows in near_rows], axis=0
    )
    near_slots = operator_cols[:, :KG]
    near_cols = (((near_slots // RB) - g) % n_grp * RB + near_slots % RB).reshape(-1)
    far_cols = operator_cols[:, KG:].reshape(-1)
    near_ids = pick_rows(near_ids_table, near_cols).reshape(RB, NEAR_E)
    far_ids = pick_rows(far_ids, relative(far_cols)).reshape(RB, FAR_E)
    live = jnp.arange(KH, dtype=jnp.int32)[None, :] < halo_count[:, None]
    spread = lambda x: jnp.repeat(x, KP, axis=0)
    near_list, near_count = match_lists(wanted, spread(near_ids), jnp.ones((PAIRS, NEAR_E), bool))
    far_live = spread(jnp.repeat(live, KP, axis=1))

    matched, left = near_call(near_cols, near_list, near_count, operator_blocks, near_rows)
    slot_shape = (HALF_C // 2 * BS, LANES)
    sources = jnp.stack([device_at(u - t, v, k, d) for t in range(SIDE)])
    owners = jnp.stack([device_at(u, v + p // 2, k + p % 2, d) for p in range(8)])
    rows_from = pick_rows(first_rows, relative(sources))
    row_of = pick_rows(rows_from.T, owners).T
    two = jnp.arange(2, dtype=jnp.int32)
    second_row = (two == 1 - row_of[0, 0])[None] & (two == 0)[:, None]

    def first_phase(half, before):
        far_list, far_count = match_lists(
            wanted[:, half * HALF_C : (half + 1) * HALF_C], spread(far_ids), far_live
        )
        chunks = far_call(
            half, far_cols, far_list, far_count, position, operator_blocks, far_rows, matched, left, n_dom
        )
        far_two = lax.ppermute(chunks[2], "dom", shift_pairs(2, 0))
        one, three, before = lax.optimization_barrier((chunks[1], chunks[3], before))
        sent = [lax.ppermute(chunk, "dom", shift_pairs(t, 0)) for t, chunk in ((1, one), (3, three))]
        return [chunks[0], sent[0], far_two, sent[1]], chunks[4], before

    def second_phase(arriving, second):
        def owned(t2):
            total = 0.0
            for t in range(SIDE):
                part = arriving[t][2 * t2 : 2 * t2 + 2][:, None]
                to_row = row_of[t, 2 * t2 : 2 * t2 + 2][:, None] == two
                total = total + jnp.where(to_row[:, :, None, None], part, 0.0)
            if t2 == 0:
                total = total + jnp.where(second_row[:, :, None, None], second[:, None], 0.0)
            return total

        sent = [lax.ppermute(owned(t2), "dom", shift_pairs(t2, 1)) for t2 in (2, 1, 3)]
        return owned(0), sent

    def swap(kept, sent):
        sums = [kept[kk] + sent[1][kk] + sent[0][kk] + sent[2][kk] for kk in (1, 0)]
        return sums[1], lax.ppermute(sums[0], "dom", [(n, n ^ 1) for n in range(n_dom)])

    arrived = []
    for half in range(HALVES):
        here, second, before = first_phase(half, arrived[-1][0] if arrived else [])
        if arrived:
            arrived[-1] = (before, arrived[-1][1])
        arrived.append((here, second))
    halves = []
    for here, second in arrived:
        if halves:
            here, _ = lax.optimization_barrier((here, halves[-1][1]))
        halves.append(second_phase(here, second))
    parts = [swap(*half) for half in halves]

    row_spec = pl.BlockSpec((1,) + slot_shape, lambda i: (i, 0, 0))
    return pl.pallas_call(
        final_kernel,
        out_shape=jax.ShapeDtypeStruct((2, KC, BS * BS), jnp.float32),
        grid=(2,),
        in_specs=[row_spec] * (2 * HALVES),
        out_specs=pl.BlockSpec((1, KC, BS * BS), lambda i: (i, 0, 0)),
        scratch_shapes=[pltpu.VMEM((KC * BS // 2, LANES), jnp.float32)],
        name="final",
    )(*[x for pair in parts for x in pair])


def solution(mesh):
    return jax.shard_map(
        per_device,
        mesh=mesh,
        in_specs=(
            P(("grp", "dom"), None, None),
            P(("grp", "dom"), None),
            P(("grp", "dom")),
            P(("grp", "dom"), None, None),
            P(("grp", "dom"), None),
            P(("grp", "dom"), None),
            P(("grp", "dom"), None),
            P(("grp", "dom"), None),
            P(("grp", "dom"), None),
        ),
        out_specs=P(("grp", "dom"), None, None),
        check_vma=False,
    )
```

```python
import functools

import jax
import jax.numpy as jnp
from jax import lax
from jax.experimental import pallas as pl
from jax.experimental.pallas import tpu as pltpu
from jax.sharding import PartitionSpec as P

BS = 64
KG = 12
KH = 4
KA = 16
KP = 8
KC = 16
RB = 4
PAIRS = RB * KP
NEAR_E = KG * KP
FAR_E = KH * KP
LANES = 128
STEP = 4
ROW_T = KP * BS * BS // LANES


def split(x):
    hi = x.astype(jnp.bfloat16)
    lo = (x - hi.astype(jnp.float32)).astype(jnp.bfloat16)
    return hi, lo


def first_half(shape):
    return lax.broadcasted_iota(jnp.int32, shape, 1) < BS


def put_right(right_ref, slot, table):
    for s in range(4):
        hi, lo = split(table(s))
        cols = slice(s * LANES, (s + 1) * LANES)
        right_ref[slot, 0:64, cols] = hi
        right_ref[slot, 64:128, cols] = hi
        right_ref[slot, 128:192, cols] = lo
        right_ref[slot, 192:256, cols] = lo


def spread_rows(a_ref, spread_ref):
    for t in range(a_ref.shape[1] // 8):
        for k in range(BS // 2):
            part = a_ref[0, t * 8 : (t + 1) * 8, k * LANES : (k + 1) * LANES]
            spread_ref[pl.ds(t * 8 * (BS // 2) + k, 8, stride=BS // 2), :] = part


def left_of(two):
    hi = two.astype(jnp.bfloat16).astype(jnp.float32)
    lo = pltpu.roll(two - hi, BS, axis=1)
    first = first_half(two.shape)
    rows = jnp.concatenate([jnp.where(first, hi, lo), jnp.where(first, lo, hi)], axis=0).astype(jnp.bfloat16)
    return jnp.concatenate([rows, rows], axis=1)


def put_weights(w_ref, m, w):
    for s in range(4):
        pair = w[:, s * LANES : (s + 1) * LANES]
        w_ref[0, m * 4 + s] = pair
        w_ref[1, m * 4 + s] = pltpu.roll(pair, BS, axis=1)


def add_matches(list_ref, base, count, w_ref, m_ref):
    half = lax.broadcasted_iota(jnp.int32, (BS, LANES), 1) // BS

    def body(k, carry):
        codes = [list_ref[base + k * STEP + t] for t in range(STEP)]
        parts = []
        for code in codes:
            e = code >> 4
            odd = code & 1
            parts.append(jnp.where(half == odd, w_ref[(e ^ code) & 1, e >> 1], 0.0))
        for code, part in zip(codes, parts):
            m_ref[(code & 15) >> 1] += part
        return carry

    lax.fori_loop(0, (count + STEP - 1) // STEP, body, 0)


def near_kernel(
    cols_ref, list_ref, count_ref, a_ref, p0, p1, p2, p3, m_ref, left_ref, right_ref, w_ref, spread_ref
):
    i = pl.program_id(0)

    @pl.when(i == 0)
    def _():
        for k, ref in enumerate((p0, p1, p2, p3)):

            def put(r, carry, k=k, ref=ref):
                def table(s):
                    return ref[pl.ds(pl.multiple_of(r * ROW_T + s * BS, BS), BS), :]

                put_right(right_ref, k * RB + r, table)
                return carry

            lax.fori_loop(0, RB, put, 0)

    for s in range(4):
        base = pl.multiple_of(i * ROW_T + s * BS, BS)
        slab = jnp.concatenate(
            [p0[pl.ds(base, BS // 2, stride=2), :], p0[pl.ds(base + 1, BS // 2, stride=2), :]], axis=0
        )
        hi = slab.astype(jnp.bfloat16).astype(jnp.float32)
        lo = slab - hi
        high = jnp.concatenate([hi, hi], axis=0).T.astype(jnp.bfloat16)
        low = jnp.concatenate([lo, lo], axis=0).T.astype(jnp.bfloat16)
        for t in range(2):
            left_ref[0, 2 * s + t, 0:BS, :] = high[t * BS : (t + 1) * BS]
            left_ref[0, 2 * s + t, BS : 2 * BS, :] = low[t * BS : (t + 1) * BS]

    for t in range(2):
        w_ref[t, NEAR_E // 2] = jnp.zeros((BS, LANES), jnp.float32)
    spread_rows(a_ref, spread_ref)
    for m in range(KG):
        left = left_of(spread_ref[m * (BS // 2) : (m + 1) * (BS // 2), :])
        w = jnp.dot(left, right_ref[cols_ref[i * KG + m]], preferred_element_type=jnp.float32)
        put_weights(w_ref, m, w)

    def per_target(j, carry):
        m_ref[0, j] = jnp.zeros((KC // 2, BS, LANES), jnp.float32)
        add_matches(list_ref, (i * KP + j) * NEAR_E, count_ref[i * KP + j], w_ref, m_ref.at[0, j])
        return carry

    lax.fori_loop(0, KP, per_target, 0)


def far_kernel(
    cols_ref, list_ref, count_ref, pos_ref, a_ref, f0, f1, f2, f3, m_ref, left_ref,
    out0, out1, out2, out3, out4, right_ref, w_ref, wide_ref, acc_ref, spread_ref, sems,
):
    i = pl.program_id(0)
    n_pos = acc_ref.shape[0]

    @pl.when(i == 0)
    def _():
        def clear(k, carry):
            acc_ref[k] = jnp.zeros(acc_ref.shape[1:], jnp.float32)
            return carry

        lax.fori_loop(0, n_pos, clear, 0)

    far = (f0, f1, f2, f3)
    for t in range(2):
        w_ref[t, FAR_E // 2] = jnp.zeros((BS, LANES), jnp.float32)
    spread_rows(a_ref, spread_ref)
    for m in range(KH):
        here = (KG % 8 + m) * (BS // 2)
        left = left_of(spread_ref[here : here + BS // 2, :])

        def table(s, m=m):
            return far[m][0, s * BS : (s + 1) * BS, :]

        put_right(right_ref, m, table)
        w = jnp.dot(left, right_ref[m], preferred_element_type=jnp.float32)
        put_weights(w_ref, m, w)

    def per_two(jj, carry):
        for t in range(2):
            j = jj * 2 + t
            here = i * KP + j
            add_matches(list_ref, here * FAR_E, count_ref[here], w_ref, m_ref.at[0, j])
        outs = []
        for t in range(2):
            j = jj * 2 + t
            for s in range(KC // 2):
                hi, lo = split(m_ref[0, j, s])
                cols = slice(s * LANES, (s + 1) * LANES)
                wide_ref[t, 0:64, cols] = hi
                wide_ref[t, 64:128, cols] = lo
            outs.append(jnp.dot(left_ref[0, j], wide_ref[t], preferred_element_type=jnp.float32))
        for t in range(2):
            pos = pos_ref[i * KP + jj * 2 + t]
            for s in range(KC // 2):
                cols = slice(s * LANES, (s + 1) * LANES)
                acc_ref[pos, s * BS : (s + 1) * BS, :] += outs[t][0:BS, cols] + outs[t][BS : 2 * BS, cols]
        return carry

    lax.fori_loop(0, KP // 2, per_two, 0)

    @pl.when(i == pl.num_programs(0) - 1)
    def _():
        copies = [
            pltpu.make_async_copy(acc_ref.at[pl.ds(k * 8, out.shape[0])], out, sems.at[k])
            for k, out in enumerate((out0, out1, out2, out3, out4))
        ]
        for copy in copies:
            copy.start()
        for copy in copies:
            copy.wait()


def final_kernel(mine_ref, got_ref, out_ref, spread_ref):
    half = BS // 2
    first = first_half((half, LANES))
    for s in range(KC // 2):
        even, odd = (pl.ds(s * BS + o, half, stride=2) for o in range(2))
        even = mine_ref[0, even, :] + got_ref[0, even, :]
        odd = mine_ref[0, odd, :] + got_ref[0, odd, :]
        spread_ref[2 * s * half : (2 * s + 1) * half, :] = jnp.where(first, even, pltpu.roll(odd, BS, axis=1))
        spread_ref[(2 * s + 1) * half : (2 * s + 2) * half, :] = jnp.where(first, pltpu.roll(even, BS, axis=1), odd)
    for t in range(KC // 8):
        for k in range(half):
            out_ref[0, t * 8 : (t + 1) * 8, k * LANES : (k + 1) * LANES] = spread_ref[
                pl.ds(t * 8 * half + k, 8, stride=half), :
            ]


def outgoing_kernel(pick_ref, blocks_ref, ids_ref, out_ref, carried_ref, spread_ref, sem):
    half = BS // 2
    first = first_half((half, LANES))

    def lay(r, carry):
        for k in range(half):
            spread_ref[pl.ds(k, KP, stride=half), :] = blocks_ref[r, :, k * LANES : (k + 1) * LANES]
        for s in range(KP // 2):
            even = spread_ref[2 * s * half : (2 * s + 1) * half, :]
            odd = spread_ref[(2 * s + 1) * half : (2 * s + 2) * half, :]
            base = r * ROW_T + s * BS
            carried_ref[pl.ds(base, half, stride=2), :] = jnp.where(first, even, pltpu.roll(odd, BS, axis=1))
            carried_ref[pl.ds(base + 1, half, stride=2), :] = jnp.where(first, pltpu.roll(even, BS, axis=1), odd)
        return carry

    lax.fori_loop(0, RB, lay, 0)
    carried_ref[RB * ROW_T : RB * ROW_T + 8, :] = jnp.zeros((8, LANES), jnp.float32)
    carried_ref[RB * ROW_T : RB * ROW_T + RB, 0:KP] = ids_ref[...].astype(jnp.float32)
    n = out_ref.shape[0]

    def copy(k):
        src = carried_ref.at[pl.ds(pl.multiple_of(pick_ref[k] * ROW_T, ROW_T), ROW_T)]
        return pltpu.make_async_copy(src, out_ref.at[k], sem.at[k])

    def start(k, carry):
        copy(k).start()
        return carry

    def wait(k, carry):
        copy(k).wait()
        return carry

    lax.fori_loop(0, n, start, 0)
    lax.fori_loop(0, n, wait, 0)


def match_lists(wanted, ids, live):
    n = ids.shape[1]
    eq = wanted[:, :, None] == ids[:, None, :]
    c_of = jnp.sum(jnp.where(eq, jnp.arange(KC, dtype=jnp.int32)[None, :, None], 0), axis=1)
    hit = jnp.any(eq, axis=1) & live
    number = jnp.arange(n, dtype=jnp.int32)
    before = jnp.sum(jnp.where((number[:, None] < number[None, :])[None], hit[:, :, None].astype(jnp.int32), 0), axis=1)
    code = number[None, :] * KC + c_of
    here = hit[:, None, :] & (before[:, None, :] == number[None, :, None])
    count = jnp.sum(hit.astype(jnp.int32), axis=1)
    lists = jnp.sum(jnp.where(here, code[:, None, :], 0), axis=2)
    lists = jnp.where(number[None, :] < count[:, None], lists, n * KC)
    return lists.reshape(-1), count


def pick_rows(table, index):
    n = table.shape[0]
    one = index[:, None] == jnp.arange(n, dtype=jnp.int32)[None, :]
    return jnp.sum(jnp.where(one[:, :, None], table[None], 0), axis=1)


def near_call(cols, lists, counts, operator_blocks, near_rows):
    row_block = pl.BlockSpec((RB * ROW_T, LANES), lambda i, *_: (0, 0))
    return pl.pallas_call(
        near_kernel,
        out_shape=(
            jax.ShapeDtypeStruct((RB, KP, KC // 2, BS, LANES), jnp.float32),
            jax.ShapeDtypeStruct((RB, KP, LANES, LANES), jnp.bfloat16),
        ),
        grid_spec=pltpu.PrefetchScalarGridSpec(
            num_scalar_prefetch=3,
            grid=(RB,),
            in_specs=[pl.BlockSpec((1, KA, BS * BS), lambda i, *_: (i, 0, 0))] + [row_block] * 4,
            out_specs=(
                pl.BlockSpec((1, KP, KC // 2, BS, LANES), lambda i, *_: (i, 0, 0, 0, 0)),
                pl.BlockSpec((1, KP, LANES, LANES), lambda i, *_: (i, 0, 0, 0)),
            ),
            scratch_shapes=[
                pltpu.VMEM((4 * RB, 256, KP * BS), jnp.bfloat16),
                pltpu.VMEM((2, NEAR_E // 2 + 1, BS, LANES), jnp.float32),
                pltpu.VMEM((KA * BS // 2, LANES), jnp.float32),
            ],
        ),
        compiler_params=pltpu.CompilerParams(vmem_limit_bytes=60 * 2**20),
        cost_estimate=pl.CostEstimate(flops=10**10, bytes_accessed=16 * 2**20, transcendentals=0),
        name="near",
    )(cols, lists, counts, operator_blocks, *near_rows)


def far_call(cols, lists, counts, position, operator_blocks, far_rows, matched, left, n_dom):
    far_spec = lambda m: pl.BlockSpec((1, ROW_T, LANES), lambda i, cols, *_: (cols[i * KH + m], 0, 0))
    slot_shape = (KC // 2 * BS, LANES)
    hbm = lambda x: pltpu.with_memory_space_constraint(x, pltpu.HBM)
    return pl.pallas_call(
        far_kernel,
        out_shape=tuple(jax.ShapeDtypeStruct((n,) + slot_shape, jnp.float32) for n in (8, 8, 8, 8, 1)),
        grid_spec=pltpu.PrefetchScalarGridSpec(
            num_scalar_prefetch=4,
            grid=(RB,),
            in_specs=[pl.BlockSpec((1, 8, BS * BS), lambda i, *_: (i, 1, 0))]
            + [far_spec(m) for m in range(KH)]
            + [
                pl.BlockSpec((1, KP, KC // 2, BS, LANES), lambda i, *_: (i, 0, 0, 0, 0)),
                pl.BlockSpec((1, KP, LANES, LANES), lambda i, *_: (i, 0, 0, 0)),
            ],
            out_specs=(pl.BlockSpec(memory_space=pltpu.HBM),) * 5,
            scratch_shapes=[
                pltpu.VMEM((KH, 256, KP * BS), jnp.bfloat16),
                pltpu.VMEM((2, FAR_E // 2 + 1, BS, LANES), jnp.float32),
                pltpu.VMEM((2, LANES, KC * BS), jnp.bfloat16),
                pltpu.VMEM((n_dom + 1,) + slot_shape, jnp.float32),
                pltpu.VMEM((8 * BS // 2, LANES), jnp.float32),
                pltpu.SemaphoreType.DMA((5,)),
            ],
        ),
        compiler_params=pltpu.CompilerParams(vmem_limit_bytes=40 * 2**20),
        cost_estimate=pl.CostEstimate(flops=10**10, bytes_accessed=24 * 2**20, transcendentals=0),
        name="far",
    )(cols, lists, counts, position, operator_blocks, *([far_rows] * KH), hbm(matched), hbm(left))


SIDE = 4


def places(device, me):
    x, y, k = device // (2 * SIDE), device // 2 % SIDE, device % 2
    return jnp.where(me % 2 == 0, x, y), jnp.where(me % 2 == 0, y, x), k


def device_at(u, v, k, me):
    u, v, k = u % SIDE, v % SIDE, k % 2
    return (jnp.where(me % 2 == 0, u, v) * SIDE + jnp.where(me % 2 == 0, v, u)) * 2 + k


def shift_pairs(shift, phase):
    pairs = []
    for x in range(SIDE):
        for y in range(SIDE):
            for k in range(2):
                along_x = (k == 0) == (phase == 0)
                to_x, to_y = ((x + shift) % SIDE, y) if along_x else (x, (y + shift) % SIDE)
                pairs.append(((x * SIDE + y) * 2 + k, (to_x * SIDE + to_y) * 2 + k))
    return pairs


def per_device(
    operator_blocks,
    operator_cols,
    halo_count,
    prolong_blocks,
    prolong_cols,
    prolong_slot,
    send_lists,
    slot_owner_row,
    coarse_pattern,
):
    n_dom = lax.axis_size("dom")
    n_grp = lax.axis_size("grp")
    g = lax.axis_index("grp")
    d = lax.axis_index("dom")
    owner = slot_owner_row.reshape(-1)

    outgoing, carried = pl.pallas_call(
        outgoing_kernel,
        out_shape=(
            jax.ShapeDtypeStruct((n_dom, ROW_T, LANES), jnp.float32),
            jax.ShapeDtypeStruct((RB * ROW_T + 8, LANES), jnp.float32),
        ),
        grid_spec=pltpu.PrefetchScalarGridSpec(
            num_scalar_prefetch=1,
            grid=(1,),
            in_specs=[
                pl.BlockSpec((RB, KP, BS * BS), lambda i, *_: (0, 0, 0)),
                pl.BlockSpec((RB, KP), lambda i, *_: (0, 0)),
            ],
            out_specs=(
                pl.BlockSpec(memory_space=pltpu.HBM),
                pl.BlockSpec((RB * ROW_T + 8, LANES), lambda i, *_: (0, 0)),
            ),
            scratch_shapes=[pltpu.VMEM((KP * BS // 2, LANES), jnp.float32), pltpu.SemaphoreType.DMA((n_dom,))],
        ),
        cost_estimate=pl.CostEstimate(flops=0, bytes_accessed=6 * 2**20, transcendentals=0),
        name="outgoing",
    )(send_lists.reshape(-1), prolong_blocks, prolong_cols)
    far_rows = lax.all_to_all(outgoing, "dom", split_axis=0, concat_axis=0, tiled=True)

    wide = lambda x: jnp.pad(x, ((0, 0), (0, 2 * n_dom - x.shape[1])))
    mine = jnp.concatenate([wide(prolong_cols), wide(coarse_pattern), wide(send_lists), slot_owner_row], axis=0)
    told = lax.all_to_all(
        jnp.broadcast_to(mine[None], (n_dom,) + mine.shape), "dom", split_axis=0, concat_axis=0, tiled=True
    )
    told, operator_cols, prolong_slot, halo_count, owner = lax.optimization_barrier(
        (told, operator_cols, prolong_slot, halo_count, owner)
    )
    all_cols = told[:, :RB, :KP]
    patterns = told[:, RB : RB + 2, :KC].reshape(2 * n_dom, KC)
    here = jnp.arange(2 * n_dom, dtype=jnp.int32)[None, :] == d
    picked = jnp.sum(jnp.where(here, told[:, RB + 2], 0), axis=1)
    slot_rows = told[:, RB + 3]
    far_ids = jnp.sum(
        jnp.where((picked[:, None] == jnp.arange(RB, dtype=jnp.int32))[:, :, None], all_cols, 0), axis=1
    )

    slots = prolong_slot.reshape(-1)
    slot_row = pick_rows(owner[:, None], slots)[:, 0]
    wanted = pick_rows(patterns, (slots // 2) * 2 + slot_row)
    u, v, k = places(d, d)
    to_u, to_v, to_k = places(slots // 2, d)
    position = ((to_u - u) % SIDE) * 8 + ((to_v - v) % SIDE) * 2 + (to_k - k) % 2
    position = jnp.where(slots % 2 == 1, n_dom, position)

    passed, _ = lax.optimization_barrier((carried, wanted))
    near_rows = [carried]
    for dz in range(1, n_grp):
        near_rows.append(lax.ppermute(passed, "grp", [((z + dz) % n_grp, z) for z in range(n_grp)]))

    near_ids_table = jnp.concatenate(
        [rows[RB * ROW_T : RB * ROW_T + RB, :KP].astype(jnp.int32) for rows in near_rows], axis=0
    )
    near_slots = operator_cols[:, :KG]
    near_cols = (((near_slots // RB) - g) % n_grp * RB + near_slots % RB).reshape(-1)
    far_cols = operator_cols[:, KG:].reshape(-1)
    near_ids = pick_rows(near_ids_table, near_cols).reshape(RB, NEAR_E)
    far_ids = pick_rows(far_ids, far_cols).reshape(RB, FAR_E)
    live = jnp.arange(KH, dtype=jnp.int32)[None, :] < halo_count[:, None]
    spread = lambda x: jnp.repeat(x, KP, axis=0)
    near_list, near_count = match_lists(wanted, spread(near_ids), jnp.ones((PAIRS, NEAR_E), bool))
    far_list, far_count = match_lists(wanted, spread(far_ids), spread(jnp.repeat(live, KP, axis=1)))

    matched, left = near_call(near_cols, near_list, near_count, operator_blocks, near_rows)
    chunks = far_call(far_cols, far_list, far_count, position, operator_blocks, far_rows, matched, left, n_dom)
    slot_shape = (KC // 2 * BS, LANES)

    sent = {t: lax.ppermute(chunks[t], "dom", shift_pairs(t, 0)) for t in (2, 1, 3)}
    *arriving, own_second = lax.optimization_barrier((chunks[0], sent[1], sent[2], sent[3], chunks[4]))
    sources = jnp.stack([device_at(u - t, v, k, d) for t in range(SIDE)])
    owners = jnp.stack([device_at(u, v + p // 2, k + p % 2, d) for p in range(8)])
    rows_from = pick_rows(slot_rows, sources)
    row_of = pick_rows(rows_from.T, 2 * owners).T
    own_first = row_of[0, 0]

    def owned(t2):
        total = 0.0
        for t in range(SIDE):
            part = arriving[t][2 * t2 : 2 * t2 + 2][:, None]
            to_row = row_of[t, 2 * t2 : 2 * t2 + 2][:, None] == jnp.arange(2, dtype=jnp.int32)
            total = total + jnp.where(to_row[:, :, None, None], part, 0.0)
        if t2 == 0:
            to_row = (jnp.arange(2, dtype=jnp.int32) == 1 - own_first)[None] & (jnp.arange(2) == 0)[:, None]
            total = total + jnp.where(to_row[:, :, None, None], own_second[:, None], 0.0)
        return total

    sent = {t2: lax.ppermute(owned(t2), "dom", shift_pairs(t2, 1)) for t2 in (2, 1, 3)}
    kept = owned(0)
    sums = [kept[kk] + sent[1][kk] + sent[2][kk] + sent[3][kk] for kk in (1, 0)]
    swapped = lax.ppermute(sums[0], "dom", [(n, n ^ 1) for n in range(n_dom)])

    row_spec = pl.BlockSpec((1,) + slot_shape, lambda i: (i, 0, 0))
    return pl.pallas_call(
        final_kernel,
        out_shape=jax.ShapeDtypeStruct((2, KC, BS * BS), jnp.float32),
        grid=(2,),
        in_specs=[row_spec, row_spec],
        out_specs=pl.BlockSpec((1, KC, BS * BS), lambda i: (i, 0, 0)),
        scratch_shapes=[pltpu.VMEM((KC * BS // 2, LANES), jnp.float32)],
        compiler_params=pltpu.CompilerParams(vmem_limit_bytes=16 * 2**20),
        name="final",
    )(sums[1], swapped)


def solution(mesh):
    return jax.shard_map(
        per_device,
        mesh=mesh,
        in_specs=(
            P(("grp", "dom"), None, None),
            P(("grp", "dom"), None),
            P(("grp", "dom")),
            P(("grp", "dom"), None, None),
            P(("grp", "dom"), None),
            P(("grp", "dom"), None),
            P(("grp", "dom"), None),
            P(("grp", "dom"), None),
            P(("grp", "dom"), None),
        ),
        out_specs=P(("grp", "dom"), None, None),
        check_vma=False,
    )
```

```python
import functools

import jax
import jax.numpy as jnp
from jax import lax
from jax.experimental import pallas as pl
from jax.experimental.pallas import tpu as pltpu
from jax.sharding import PartitionSpec as P

BS = 64
KG = 12
KH = 4
KA = 16
KP = 8
KC = 16
HALVES = 2
HALF_C = KC // HALVES
RB = 4
PAIRS = RB * KP
NEAR_E = KG * KP
FAR_E = KH * KP
LANES = 128
STEP = 4
ROW_T = KP * BS * BS // LANES


def split(x):
    hi = x.astype(jnp.bfloat16)
    lo = (x - hi.astype(jnp.float32)).astype(jnp.bfloat16)
    return hi, lo


def first_half(shape):
    return lax.broadcasted_iota(jnp.int32, shape, 1) < BS


def put_right(right_ref, slot, table):
    for s in range(4):
        hi, lo = split(table(s))
        cols = slice(s * LANES, (s + 1) * LANES)
        right_ref[slot, 0:64, cols] = hi
        right_ref[slot, 64:128, cols] = hi
        right_ref[slot, 128:192, cols] = lo
        right_ref[slot, 192:256, cols] = lo


def spread_rows(a_ref, spread_ref):
    for t in range(a_ref.shape[1] // 8):
        for k in range(BS // 2):
            part = a_ref[0, t * 8 : (t + 1) * 8, k * LANES : (k + 1) * LANES]
            spread_ref[pl.ds(t * 8 * (BS // 2) + k, 8, stride=BS // 2), :] = part


def left_of(two):
    hi = two.astype(jnp.bfloat16).astype(jnp.float32)
    lo = pltpu.roll(two - hi, BS, axis=1)
    first = first_half(two.shape)
    rows = jnp.concatenate([jnp.where(first, hi, lo), jnp.where(first, lo, hi)], axis=0).astype(jnp.bfloat16)
    return jnp.concatenate([rows, rows], axis=1)


def put_weights(w_ref, m, w):
    for s in range(4):
        pair = w[:, s * LANES : (s + 1) * LANES]
        w_ref[0, m * 4 + s] = pair
        w_ref[1, m * 4 + s] = pltpu.roll(pair, BS, axis=1)


def add_matches(list_ref, base, count, w_ref, m_ref):
    half = lax.broadcasted_iota(jnp.int32, (BS, LANES), 1) // BS

    def body(k, carry):
        codes = [list_ref[base + k * STEP + t] for t in range(STEP)]
        parts = []
        for code in codes:
            e = code >> 4
            odd = code & 1
            parts.append(jnp.where(half == odd, w_ref[(e ^ code) & 1, e >> 1], 0.0))
        for code, part in zip(codes, parts):
            m_ref[(code & 15) >> 1] += part
        return carry

    lax.fori_loop(0, (count + STEP - 1) // STEP, body, 0)


def near_kernel(
    cols_ref, list_ref, count_ref, a_ref, p0, p1, p2, p3, m_ref, left_ref, right_ref, w_ref, spread_ref
):
    i = pl.program_id(0)

    @pl.when(i == 0)
    def _():
        for k, ref in enumerate((p0, p1, p2, p3)):

            def put(r, carry, k=k, ref=ref):
                def table(s):
                    return ref[pl.ds(pl.multiple_of(r * ROW_T + s * BS, BS), BS), :]

                put_right(right_ref, k * RB + r, table)
                return carry

            lax.fori_loop(0, RB, put, 0)

    for s in range(4):
        base = pl.multiple_of(i * ROW_T + s * BS, BS)
        slab = jnp.concatenate(
            [p0[pl.ds(base, BS // 2, stride=2), :], p0[pl.ds(base + 1, BS // 2, stride=2), :]], axis=0
        )
        hi = slab.astype(jnp.bfloat16).astype(jnp.float32)
        lo = slab - hi
        high = jnp.concatenate([hi, hi], axis=0).T.astype(jnp.bfloat16)
        low = jnp.concatenate([lo, lo], axis=0).T.astype(jnp.bfloat16)
        for t in range(2):
            left_ref[0, 2 * s + t, 0:BS, :] = high[t * BS : (t + 1) * BS]
            left_ref[0, 2 * s + t, BS : 2 * BS, :] = low[t * BS : (t + 1) * BS]

    for t in range(2):
        w_ref[t, NEAR_E // 2] = jnp.zeros((BS, LANES), jnp.float32)
    spread_rows(a_ref, spread_ref)
    for m in range(KG):
        left = left_of(spread_ref[m * (BS // 2) : (m + 1) * (BS // 2), :])
        w = jnp.dot(left, right_ref[cols_ref[i * KG + m]], preferred_element_type=jnp.float32)
        put_weights(w_ref, m, w)

    def per_target(j, carry):
        m_ref[0, j] = jnp.zeros((KC // 2, BS, LANES), jnp.float32)
        add_matches(list_ref, (i * KP + j) * NEAR_E, count_ref[i * KP + j], w_ref, m_ref.at[0, j])
        return carry

    lax.fori_loop(0, KP, per_target, 0)


def far_kernel(
    cols_ref, list_ref, count_ref, pos_ref, a_ref, f0, f1, f2, f3, m_ref, left_ref,
    out0, out1, out2, out3, out4, right_ref, w_ref, wide_ref, acc_ref, spread_ref, sems,
):
    i = pl.program_id(0)
    n_pos = acc_ref.shape[0]

    @pl.when(i == 0)
    def _():
        def clear(k, carry):
            acc_ref[k] = jnp.zeros(acc_ref.shape[1:], jnp.float32)
            return carry

        lax.fori_loop(0, n_pos, clear, 0)

    far = (f0, f1, f2, f3)
    for t in range(2):
        w_ref[t, FAR_E // 2] = jnp.zeros((BS, LANES), jnp.float32)
    spread_rows(a_ref, spread_ref)
    for m in range(KH):
        here = (KG % 8 + m) * (BS // 2)
        left = left_of(spread_ref[here : here + BS // 2, :])

        def table(s, m=m):
            return far[m][0, s * BS : (s + 1) * BS, :]

        put_right(right_ref, m, table)
        w = jnp.dot(left, right_ref[m], preferred_element_type=jnp.float32)
        put_weights(w_ref, m, w)

    def per_two(jj, carry):
        for t in range(2):
            j = jj * 2 + t
            here = i * KP + j
            add_matches(list_ref, here * FAR_E, count_ref[here], w_ref, m_ref.at[0, j])
        outs = []
        for t in range(2):
            j = jj * 2 + t
            for s in range(HALF_C // 2):
                hi, lo = split(m_ref[0, j, s])
                cols = slice(s * LANES, (s + 1) * LANES)
                wide_ref[t, 0:64, cols] = hi
                wide_ref[t, 64:128, cols] = lo
            outs.append(jnp.dot(left_ref[0, j], wide_ref[t], preferred_element_type=jnp.float32))
        for t in range(2):
            pos = pos_ref[i * KP + jj * 2 + t]
            for s in range(HALF_C // 2):
                cols = slice(s * LANES, (s + 1) * LANES)
                acc_ref[pos, s * BS : (s + 1) * BS, :] += outs[t][0:BS, cols] + outs[t][BS : 2 * BS, cols]
        return carry

    lax.fori_loop(0, KP // 2, per_two, 0)

    @pl.when(i == pl.num_programs(0) - 1)
    def _():
        copies = [
            pltpu.make_async_copy(acc_ref.at[pl.ds(k * 8, out.shape[0])], out, sems.at[k])
            for k, out in enumerate((out0, out1, out2, out3, out4))
        ]
        for copy in copies:
            copy.start()
        for copy in copies:
            copy.wait()


def final_kernel(*refs):
    *parts, out_ref, spread_ref = refs
    half = BS // 2
    first = first_half((half, LANES))
    for s in range(KC // 2):
        mine_ref, got_ref = parts[2 * (s // (HALF_C // 2)) : 2 * (s // (HALF_C // 2)) + 2]
        even, odd = (pl.ds(s % (HALF_C // 2) * BS + o, half, stride=2) for o in range(2))
        even = mine_ref[0, even, :] + got_ref[0, even, :]
        odd = mine_ref[0, odd, :] + got_ref[0, odd, :]
        spread_ref[2 * s * half : (2 * s + 1) * half, :] = jnp.where(first, even, pltpu.roll(odd, BS, axis=1))
        spread_ref[(2 * s + 1) * half : (2 * s + 2) * half, :] = jnp.where(first, pltpu.roll(even, BS, axis=1), odd)
    for t in range(KC // 8):
        for k in range(half):
            out_ref[0, t * 8 : (t + 1) * 8, k * LANES : (k + 1) * LANES] = spread_ref[
                pl.ds(t * 8 * half + k, 8, stride=half), :
            ]


def outgoing_kernel(pick_ref, blocks_ref, ids_ref, out_ref, carried_ref, spread_ref, sem):
    half = BS // 2
    first = first_half((half, LANES))

    def lay(r, carry):
        for k in range(half):
            spread_ref[pl.ds(k, KP, stride=half), :] = blocks_ref[r, :, k * LANES : (k + 1) * LANES]
        for s in range(KP // 2):
            even = spread_ref[2 * s * half : (2 * s + 1) * half, :]
            odd = spread_ref[(2 * s + 1) * half : (2 * s + 2) * half, :]
            base = r * ROW_T + s * BS
            carried_ref[pl.ds(base, half, stride=2), :] = jnp.where(first, even, pltpu.roll(odd, BS, axis=1))
            carried_ref[pl.ds(base + 1, half, stride=2), :] = jnp.where(first, pltpu.roll(even, BS, axis=1), odd)
        return carry

    lax.fori_loop(0, RB, lay, 0)
    carried_ref[RB * ROW_T : RB * ROW_T + 8, :] = jnp.zeros((8, LANES), jnp.float32)
    carried_ref[RB * ROW_T : RB * ROW_T + RB, 0:KP] = ids_ref[...].astype(jnp.float32)
    n = out_ref.shape[0]

    def copy(k):
        src = carried_ref.at[pl.ds(pl.multiple_of(pick_ref[k] * ROW_T, ROW_T), ROW_T)]
        return pltpu.make_async_copy(src, out_ref.at[k], sem.at[k])

    def start(k, carry):
        copy(k).start()
        return carry

    def wait(k, carry):
        copy(k).wait()
        return carry

    lax.fori_loop(0, n, start, 0)
    lax.fori_loop(0, n, wait, 0)


def match_lists(wanted, ids, live):
    n = ids.shape[1]
    eq = wanted[:, :, None] == ids[:, None, :]
    c_of = jnp.sum(jnp.where(eq, jnp.arange(wanted.shape[1], dtype=jnp.int32)[None, :, None], 0), axis=1)
    hit = jnp.any(eq, axis=1) & live
    number = jnp.arange(n, dtype=jnp.int32)
    before = jnp.sum(jnp.where((number[:, None] < number[None, :])[None], hit[:, :, None].astype(jnp.int32), 0), axis=1)
    code = number[None, :] * KC + c_of
    here = hit[:, None, :] & (before[:, None, :] == number[None, :, None])
    count = jnp.sum(hit.astype(jnp.int32), axis=1)
    lists = jnp.sum(jnp.where(here, code[:, None, :], 0), axis=2)
    lists = jnp.where(number[None, :] < count[:, None], lists, n * KC)
    return lists.reshape(-1), count


def pick_rows(table, index):
    n = table.shape[0]
    one = index[:, None] == jnp.arange(n, dtype=jnp.int32)[None, :]
    return jnp.sum(jnp.where(one[:, :, None], table[None], 0), axis=1)


def near_call(cols, lists, counts, operator_blocks, near_rows):
    row_block = pl.BlockSpec((RB * ROW_T, LANES), lambda i, *_: (0, 0))
    return pl.pallas_call(
        near_kernel,
        out_shape=(
            jax.ShapeDtypeStruct((RB, KP, KC // 2, BS, LANES), jnp.float32),
            jax.ShapeDtypeStruct((RB, KP, LANES, LANES), jnp.bfloat16),
        ),
        grid_spec=pltpu.PrefetchScalarGridSpec(
            num_scalar_prefetch=3,
            grid=(RB,),
            in_specs=[pl.BlockSpec((1, KA, BS * BS), lambda i, *_: (i, 0, 0))] + [row_block] * 4,
            out_specs=(
                pl.BlockSpec((1, KP, KC // 2, BS, LANES), lambda i, *_: (i, 0, 0, 0, 0)),
                pl.BlockSpec((1, KP, LANES, LANES), lambda i, *_: (i, 0, 0, 0)),
            ),
            scratch_shapes=[
                pltpu.VMEM((4 * RB, 256, KP * BS), jnp.bfloat16),
                pltpu.VMEM((2, NEAR_E // 2 + 1, BS, LANES), jnp.float32),
                pltpu.VMEM((KA * BS // 2, LANES), jnp.float32),
            ],
        ),
        compiler_params=pltpu.CompilerParams(vmem_limit_bytes=60 * 2**20),
        cost_estimate=pl.CostEstimate(flops=10**10, bytes_accessed=16 * 2**20, transcendentals=0),
        name="near",
    )(cols, lists, counts, operator_blocks, *near_rows)


def far_call(half, cols, lists, counts, position, operator_blocks, far_rows, matched, left, n_dom):
    far_spec = lambda m: pl.BlockSpec((1, ROW_T, LANES), lambda i, cols, *_: (cols[i * KH + m], 0, 0))
    slot_shape = (HALF_C // 2 * BS, LANES)
    hbm = lambda x: pltpu.with_memory_space_constraint(x, pltpu.HBM)
    return pl.pallas_call(
        far_kernel,
        out_shape=tuple(jax.ShapeDtypeStruct((n,) + slot_shape, jnp.float32) for n in (8, 8, 8, 8, 1)),
        grid_spec=pltpu.PrefetchScalarGridSpec(
            num_scalar_prefetch=4,
            grid=(RB,),
            in_specs=[pl.BlockSpec((1, 8, BS * BS), lambda i, *_: (i, 1, 0))]
            + [far_spec(m) for m in range(KH)]
            + [
                pl.BlockSpec((1, KP, HALF_C // 2, BS, LANES), lambda i, *_: (i, 0, half, 0, 0)),
                pl.BlockSpec((1, KP, LANES, LANES), lambda i, *_: (i, 0, 0, 0)),
            ],
            out_specs=(pl.BlockSpec(memory_space=pltpu.HBM),) * 5,
            scratch_shapes=[
                pltpu.VMEM((KH, 256, KP * BS), jnp.bfloat16),
                pltpu.VMEM((2, FAR_E // 2 + 1, BS, LANES), jnp.float32),
                pltpu.VMEM((2, LANES, HALF_C * BS), jnp.bfloat16),
                pltpu.VMEM((n_dom + 1,) + slot_shape, jnp.float32),
                pltpu.VMEM((8 * BS // 2, LANES), jnp.float32),
                pltpu.SemaphoreType.DMA((5,)),
            ],
        ),
        compiler_params=pltpu.CompilerParams(vmem_limit_bytes=40 * 2**20),
        cost_estimate=pl.CostEstimate(flops=5 * 10**9, bytes_accessed=14 * 2**20, transcendentals=0),
        name="far",
    )(cols, lists, counts, position, operator_blocks, *([far_rows] * KH), hbm(matched), hbm(left))


SIDE = 4


def places(device, me):
    x, y, k = device // (2 * SIDE), device // 2 % SIDE, device % 2
    return jnp.where(me % 2 == 0, x, y), jnp.where(me % 2 == 0, y, x), k


def device_at(u, v, k, me):
    u, v, k = u % SIDE, v % SIDE, k % 2
    return (jnp.where(me % 2 == 0, u, v) * SIDE + jnp.where(me % 2 == 0, v, u)) * 2 + k


def shift_pairs(shift, phase):
    pairs = []
    for x in range(SIDE):
        for y in range(SIDE):
            for k in range(2):
                along_x = (k == 0) == (phase == 0)
                to_x, to_y = ((x + shift) % SIDE, y) if along_x else (x, (y + shift) % SIDE)
                pairs.append(((x * SIDE + y) * 2 + k, (to_x * SIDE + to_y) * 2 + k))
    return pairs


def per_device(
    operator_blocks,
    operator_cols,
    halo_count,
    prolong_blocks,
    prolong_cols,
    prolong_slot,
    send_lists,
    slot_owner_row,
    coarse_pattern,
):
    n_dom = lax.axis_size("dom")
    n_grp = lax.axis_size("grp")
    g = lax.axis_index("grp")
    d = lax.axis_index("dom")
    owner = slot_owner_row.reshape(-1)

    outgoing, carried = pl.pallas_call(
        outgoing_kernel,
        out_shape=(
            jax.ShapeDtypeStruct((n_dom, ROW_T, LANES), jnp.float32),
            jax.ShapeDtypeStruct((RB * ROW_T + 8, LANES), jnp.float32),
        ),
        grid_spec=pltpu.PrefetchScalarGridSpec(
            num_scalar_prefetch=1,
            grid=(1,),
            in_specs=[
                pl.BlockSpec((RB, KP, BS * BS), lambda i, *_: (0, 0, 0)),
                pl.BlockSpec((RB, KP), lambda i, *_: (0, 0)),
            ],
            out_specs=(
                pl.BlockSpec(memory_space=pltpu.HBM),
                pl.BlockSpec((RB * ROW_T + 8, LANES), lambda i, *_: (0, 0)),
            ),
            scratch_shapes=[pltpu.VMEM((KP * BS // 2, LANES), jnp.float32), pltpu.SemaphoreType.DMA((n_dom,))],
        ),
        cost_estimate=pl.CostEstimate(flops=0, bytes_accessed=6 * 2**20, transcendentals=0),
        name="outgoing",
    )(send_lists.reshape(-1), prolong_blocks, prolong_cols)
    far_rows = lax.all_to_all(outgoing, "dom", split_axis=0, concat_axis=0, tiled=True)

    wide = lambda x: jnp.pad(x, ((0, 0), (0, 2 * n_dom - x.shape[1])))
    mine = jnp.concatenate([wide(prolong_cols), wide(coarse_pattern), wide(send_lists), slot_owner_row], axis=0)
    told = lax.all_to_all(
        jnp.broadcast_to(mine[None], (n_dom,) + mine.shape), "dom", split_axis=0, concat_axis=0, tiled=True
    )
    told, operator_cols, prolong_slot, halo_count, owner = lax.optimization_barrier(
        (told, operator_cols, prolong_slot, halo_count, owner)
    )
    all_cols = told[:, :RB, :KP]
    patterns = told[:, RB : RB + 2, :KC].reshape(2 * n_dom, KC)
    here = jnp.arange(2 * n_dom, dtype=jnp.int32)[None, :] == d
    picked = jnp.sum(jnp.where(here, told[:, RB + 2], 0), axis=1)
    slot_rows = told[:, RB + 3]
    far_ids = jnp.sum(
        jnp.where((picked[:, None] == jnp.arange(RB, dtype=jnp.int32))[:, :, None], all_cols, 0), axis=1
    )

    slots = prolong_slot.reshape(-1)
    slot_row = pick_rows(owner[:, None], slots)[:, 0]
    wanted = pick_rows(patterns, (slots // 2) * 2 + slot_row)
    u, v, k = places(d, d)
    to_u, to_v, to_k = places(slots // 2, d)
    position = ((to_u - u) % SIDE) * 8 + ((to_v - v) % SIDE) * 2 + (to_k - k) % 2
    position = jnp.where(slots % 2 == 1, n_dom, position)

    passed, _ = lax.optimization_barrier((carried, wanted))
    near_rows = [carried]
    for dz in range(1, n_grp):
        near_rows.append(lax.ppermute(passed, "grp", [((z + dz) % n_grp, z) for z in range(n_grp)]))

    near_ids_table = jnp.concatenate(
        [rows[RB * ROW_T : RB * ROW_T + RB, :KP].astype(jnp.int32) for rows in near_rows], axis=0
    )
    near_slots = operator_cols[:, :KG]
    near_cols = (((near_slots // RB) - g) % n_grp * RB + near_slots % RB).reshape(-1)
    far_cols = operator_cols[:, KG:].reshape(-1)
    near_ids = pick_rows(near_ids_table, near_cols).reshape(RB, NEAR_E)
    far_ids = pick_rows(far_ids, far_cols).reshape(RB, FAR_E)
    live = jnp.arange(KH, dtype=jnp.int32)[None, :] < halo_count[:, None]
    spread = lambda x: jnp.repeat(x, KP, axis=0)
    near_list, near_count = match_lists(wanted, spread(near_ids), jnp.ones((PAIRS, NEAR_E), bool))
    far_live = spread(jnp.repeat(live, KP, axis=1))
    far_lists = [
        match_lists(wanted[:, half * HALF_C : (half + 1) * HALF_C], spread(far_ids), far_live) for half in range(HALVES)
    ]

    matched, left = near_call(near_cols, near_list, near_count, operator_blocks, near_rows)
    slot_shape = (HALF_C // 2 * BS, LANES)
    sources = jnp.stack([device_at(u - t, v, k, d) for t in range(SIDE)])
    owners = jnp.stack([device_at(u, v + p // 2, k + p % 2, d) for p in range(8)])
    rows_from = pick_rows(slot_rows, sources)
    row_of = pick_rows(rows_from.T, 2 * owners).T
    two = jnp.arange(2, dtype=jnp.int32)
    second_row = (two == 1 - row_of[0, 0])[None] & (two == 0)[:, None]

    def first_phase(half):
        far_list, far_count = far_lists[half]
        chunks = far_call(
            half, far_cols, far_list, far_count, position, operator_blocks, far_rows, matched, left, n_dom
        )
        sent = {t: lax.ppermute(chunks[t], "dom", shift_pairs(t, 0)) for t in (2, 1, 3)}
        return lax.optimization_barrier((chunks[0], sent[1], sent[2], sent[3], chunks[4]))

    def second_phase(here):
        *arriving, second = here

        def owned(t2):
            total = 0.0
            for t in range(SIDE):
                part = arriving[t][2 * t2 : 2 * t2 + 2][:, None]
                to_row = row_of[t, 2 * t2 : 2 * t2 + 2][:, None] == two
                total = total + jnp.where(to_row[:, :, None, None], part, 0.0)
            if t2 == 0:
                total = total + jnp.where(second_row[:, :, None, None], second[:, None], 0.0)
            return total

        sent = [lax.ppermute(owned(t2), "dom", shift_pairs(t2, 1)) for t2 in (2, 1, 3)]
        return owned(0), sent

    def swap(kept, sent):
        sums = [kept[kk] + sent[1][kk] + sent[0][kk] + sent[2][kk] for kk in (1, 0)]
        return sums[1], lax.ppermute(sums[0], "dom", [(n, n ^ 1) for n in range(n_dom)])

    arrived = [first_phase(half) for half in range(HALVES)]
    halves = [second_phase(here) for here in arrived]
    parts = [swap(*half) for half in halves]

    row_spec = pl.BlockSpec((1,) + slot_shape, lambda i: (i, 0, 0))
    return pl.pallas_call(
        final_kernel,
        out_shape=jax.ShapeDtypeStruct((2, KC, BS * BS), jnp.float32),
        grid=(2,),
        in_specs=[row_spec] * (2 * HALVES),
        out_specs=pl.BlockSpec((1, KC, BS * BS), lambda i: (i, 0, 0)),
        scratch_shapes=[pltpu.VMEM((KC * BS // 2, LANES), jnp.float32)],
        compiler_params=pltpu.CompilerParams(vmem_limit_bytes=16 * 2**20),
        name="final",
    )(*[x for pair in parts for x in pair])


def solution(mesh):
    return jax.shard_map(
        per_device,
        mesh=mesh,
        in_specs=(
            P(("grp", "dom"), None, None),
            P(("grp", "dom"), None),
            P(("grp", "dom")),
            P(("grp", "dom"), None, None),
            P(("grp", "dom"), None),
            P(("grp", "dom"), None),
            P(("grp", "dom"), None),
            P(("grp", "dom"), None),
            P(("grp", "dom"), None),
        ),
        out_specs=P(("grp", "dom"), None, None),
        check_vma=False,
    )
```

```python
import functools

import jax
import jax.numpy as jnp
from jax import lax
from jax.experimental import pallas as pl
from jax.experimental.pallas import tpu as pltpu
from jax.sharding import PartitionSpec as P

BS = 64
KG = 12
KH = 4
KA = 16
KP = 8
KC = 16
HALVES = 2
HALF_C = KC // HALVES
RB = 4
PAIRS = RB * KP
NEAR_E = KG * KP
FAR_E = KH * KP
LANES = 128
STEP = 4
ROW_T = KP * BS * BS // LANES


def split(x):
    hi = x.astype(jnp.bfloat16)
    lo = (x - hi.astype(jnp.float32)).astype(jnp.bfloat16)
    return hi, lo


def first_half(shape):
    return lax.broadcasted_iota(jnp.int32, shape, 1) < BS


def put_right(right_ref, slot, table):
    for s in range(4):
        hi, lo = split(table(s))
        cols = slice(s * LANES, (s + 1) * LANES)
        right_ref[slot, 0:64, cols] = hi
        right_ref[slot, 64:128, cols] = lo


def spread_rows(a_ref, spread_ref):
    for t in range(a_ref.shape[1] // 8):
        for k in range(BS // 2):
            part = a_ref[0, t * 8 : (t + 1) * 8, k * LANES : (k + 1) * LANES]
            spread_ref[pl.ds(t * 8 * (BS // 2) + k, 8, stride=BS // 2), :] = part


def left_of(two):
    other = pltpu.roll(two, BS, axis=1)
    first = first_half(two.shape)
    rows = jnp.concatenate([jnp.where(first, two, other), jnp.where(first, other, two)], axis=0)
    return jnp.concatenate(split(rows), axis=0)


def weights_of(left, right):
    both = jnp.dot(left, right, preferred_element_type=jnp.float32)
    return both[0:BS] + both[BS : 2 * BS]


def put_weights(w_ref, m, w):
    for s in range(4):
        pair = w[:, s * LANES : (s + 1) * LANES]
        w_ref[0, m * 4 + s] = pair
        w_ref[1, m * 4 + s] = pltpu.roll(pair, BS, axis=1)


def add_matches(list_ref, base, count, w_ref, m_ref):
    half = lax.broadcasted_iota(jnp.int32, (BS, LANES), 1) // BS

    def body(k, carry):
        codes = [list_ref[base + k * STEP + t] for t in range(STEP)]
        parts = []
        for code in codes:
            e = code >> 4
            odd = code & 1
            parts.append(jnp.where(half == odd, w_ref[(e ^ code) & 1, e >> 1], 0.0))
        for code, part in zip(codes, parts):
            m_ref[(code & 15) >> 1] += part
        return carry

    lax.fori_loop(0, (count + STEP - 1) // STEP, body, 0)


def near_kernel(
    cols_ref, list_ref, count_ref, a_ref, p0, p1, p2, p3, m_ref, left_ref, right_ref, w_ref, spread_ref
):
    i = pl.program_id(0)

    @pl.when(i == 0)
    def _():
        for k, ref in enumerate((p0, p1, p2, p3)):

            def put(r, carry, k=k, ref=ref):
                def table(s):
                    return ref[pl.ds(pl.multiple_of(r * ROW_T + s * BS, BS), BS), :]

                put_right(right_ref, k * RB + r, table)
                return carry

            lax.fori_loop(0, RB, put, 0)

    for s in range(4):
        base = pl.multiple_of(i * ROW_T + s * BS, BS)
        slab = jnp.concatenate(
            [p0[pl.ds(base, BS // 2, stride=2), :], p0[pl.ds(base + 1, BS // 2, stride=2), :]], axis=0
        )
        hi = slab.astype(jnp.bfloat16).astype(jnp.float32)
        lo = slab - hi
        high = jnp.concatenate([hi, hi], axis=0).T.astype(jnp.bfloat16)
        low = jnp.concatenate([lo, lo], axis=0).T.astype(jnp.bfloat16)
        for t in range(2):
            left_ref[0, 2 * s + t, 0:BS, :] = high[t * BS : (t + 1) * BS]
            left_ref[0, 2 * s + t, BS : 2 * BS, :] = low[t * BS : (t + 1) * BS]

    for t in range(2):
        w_ref[t, NEAR_E // 2] = jnp.zeros((BS, LANES), jnp.float32)
    spread_rows(a_ref, spread_ref)
    for m in range(KG):
        left = left_of(spread_ref[m * (BS // 2) : (m + 1) * (BS // 2), :])
        w = weights_of(left, right_ref[cols_ref[i * KG + m]])
        put_weights(w_ref, m, w)

    def per_target(j, carry):
        m_ref[0, j] = jnp.zeros((KC // 2, BS, LANES), jnp.float32)
        add_matches(list_ref, (i * KP + j) * NEAR_E, count_ref[i * KP + j], w_ref, m_ref.at[0, j])
        return carry

    lax.fori_loop(0, KP, per_target, 0)


def far_kernel(
    cols_ref, list_ref, count_ref, pos_ref, a_ref, f0, f1, f2, f3, m_ref, left_ref,
    out0, out1, out2, out3, out4, right_ref, w_ref, wide_ref, acc_ref, spread_ref, sems,
):
    i = pl.program_id(0)
    n_pos = acc_ref.shape[0]

    @pl.when(i == 0)
    def _():
        def clear(k, carry):
            acc_ref[k] = jnp.zeros(acc_ref.shape[1:], jnp.float32)
            return carry

        lax.fori_loop(0, n_pos, clear, 0)

    far = (f0, f1, f2, f3)
    for t in range(2):
        w_ref[t, FAR_E // 2] = jnp.zeros((BS, LANES), jnp.float32)
    spread_rows(a_ref, spread_ref)
    for m in range(KH):
        here = (KG % 8 + m) * (BS // 2)
        left = left_of(spread_ref[here : here + BS // 2, :])

        def table(s, m=m):
            return far[m][0, s * BS : (s + 1) * BS, :]

        put_right(right_ref, m, table)
        w = weights_of(left, right_ref[m])
        put_weights(w_ref, m, w)

    def per_two(jj, carry):
        for t in range(2):
            j = jj * 2 + t
            here = i * KP + j
            add_matches(list_ref, here * FAR_E, count_ref[here], w_ref, m_ref.at[0, j])
        outs = []
        for t in range(2):
            j = jj * 2 + t
            for s in range(HALF_C // 2):
                hi, lo = split(m_ref[0, j, s])
                cols = slice(s * LANES, (s + 1) * LANES)
                wide_ref[t, 0:64, cols] = hi
                wide_ref[t, 64:128, cols] = lo
            outs.append(jnp.dot(left_ref[0, j], wide_ref[t], preferred_element_type=jnp.float32))
        for t in range(2):
            pos = pos_ref[i * KP + jj * 2 + t]
            for s in range(HALF_C // 2):
                cols = slice(s * LANES, (s + 1) * LANES)
                acc_ref[pos, s * BS : (s + 1) * BS, :] += outs[t][0:BS, cols] + outs[t][BS : 2 * BS, cols]
        return carry

    lax.fori_loop(0, KP // 2, per_two, 0)

    @pl.when(i == pl.num_programs(0) - 1)
    def _():
        copies = [
            pltpu.make_async_copy(acc_ref.at[pl.ds(k * 8, out.shape[0])], out, sems.at[k])
            for k, out in enumerate((out0, out1, out2, out3, out4))
        ]
        for copy in copies:
            copy.start()
        for copy in copies:
            copy.wait()


def final_kernel(*refs):
    *parts, out_ref, spread_ref = refs
    half = BS // 2
    first = first_half((half, LANES))
    for s in range(KC // 2):
        mine_ref, got_ref = parts[2 * (s // (HALF_C // 2)) : 2 * (s // (HALF_C // 2)) + 2]
        even, odd = (pl.ds(s % (HALF_C // 2) * BS + o, half, stride=2) for o in range(2))
        even = mine_ref[0, even, :] + got_ref[0, even, :]
        odd = mine_ref[0, odd, :] + got_ref[0, odd, :]
        spread_ref[2 * s * half : (2 * s + 1) * half, :] = jnp.where(first, even, pltpu.roll(odd, BS, axis=1))
        spread_ref[(2 * s + 1) * half : (2 * s + 2) * half, :] = jnp.where(first, pltpu.roll(even, BS, axis=1), odd)
    for t in range(KC // 8):
        for k in range(half):
            out_ref[0, t * 8 : (t + 1) * 8, k * LANES : (k + 1) * LANES] = spread_ref[
                pl.ds(t * 8 * half + k, 8, stride=half), :
            ]


def outgoing_kernel(pick_ref, blocks_ref, ids_ref, out_ref, carried_ref, spread_ref, sem):
    half = BS // 2
    first = first_half((half, LANES))

    def lay(r, carry):
        for k in range(half):
            spread_ref[pl.ds(k, KP, stride=half), :] = blocks_ref[r, :, k * LANES : (k + 1) * LANES]
        for s in range(KP // 2):
            even = spread_ref[2 * s * half : (2 * s + 1) * half, :]
            odd = spread_ref[(2 * s + 1) * half : (2 * s + 2) * half, :]
            base = r * ROW_T + s * BS
            carried_ref[pl.ds(base, half, stride=2), :] = jnp.where(first, even, pltpu.roll(odd, BS, axis=1))
            carried_ref[pl.ds(base + 1, half, stride=2), :] = jnp.where(first, pltpu.roll(even, BS, axis=1), odd)
        return carry

    lax.fori_loop(0, RB, lay, 0)
    carried_ref[RB * ROW_T : RB * ROW_T + 8, :] = jnp.zeros((8, LANES), jnp.float32)
    carried_ref[RB * ROW_T : RB * ROW_T + RB, 0:KP] = ids_ref[...].astype(jnp.float32)
    n = out_ref.shape[0]

    def copy(k):
        src = carried_ref.at[pl.ds(pl.multiple_of(pick_ref[k] * ROW_T, ROW_T), ROW_T)]
        return pltpu.make_async_copy(src, out_ref.at[k], sem.at[k])

    def start(k, carry):
        copy(k).start()
        return carry

    def wait(k, carry):
        copy(k).wait()
        return carry

    lax.fori_loop(0, n, start, 0)
    lax.fori_loop(0, n, wait, 0)


def match_lists(wanted, ids, live):
    n = ids.shape[1]
    eq = wanted[:, :, None] == ids[:, None, :]
    c_of = jnp.sum(jnp.where(eq, jnp.arange(wanted.shape[1], dtype=jnp.int32)[None, :, None], 0), axis=1)
    hit = jnp.any(eq, axis=1) & live
    number = jnp.arange(n, dtype=jnp.int32)
    before = jnp.sum(jnp.where((number[:, None] < number[None, :])[None], hit[:, :, None].astype(jnp.int32), 0), axis=1)
    code = number[None, :] * KC + c_of
    here = hit[:, None, :] & (before[:, None, :] == number[None, :, None])
    count = jnp.sum(hit.astype(jnp.int32), axis=1)
    lists = jnp.sum(jnp.where(here, code[:, None, :], 0), axis=2)
    lists = jnp.where(number[None, :] < count[:, None], lists, n * KC)
    return lists.reshape(-1), count


def pick_rows(table, index):
    n = table.shape[0]
    one = index[:, None] == jnp.arange(n, dtype=jnp.int32)[None, :]
    return jnp.sum(jnp.where(one[:, :, None], table[None], 0), axis=1)


def near_call(cols, lists, counts, operator_blocks, near_rows):
    row_block = pl.BlockSpec((RB * ROW_T, LANES), lambda i, *_: (0, 0))
    return pl.pallas_call(
        near_kernel,
        out_shape=(
            jax.ShapeDtypeStruct((RB, KP, KC // 2, BS, LANES), jnp.float32),
            jax.ShapeDtypeStruct((RB, KP, LANES, LANES), jnp.bfloat16),
        ),
        grid_spec=pltpu.PrefetchScalarGridSpec(
            num_scalar_prefetch=3,
            grid=(RB,),
            in_specs=[pl.BlockSpec((1, KA, BS * BS), lambda i, *_: (i, 0, 0))] + [row_block] * 4,
            out_specs=(
                pl.BlockSpec((1, KP, KC // 2, BS, LANES), lambda i, *_: (i, 0, 0, 0, 0)),
                pl.BlockSpec((1, KP, LANES, LANES), lambda i, *_: (i, 0, 0, 0)),
            ),
            scratch_shapes=[
                pltpu.VMEM((4 * RB, LANES, KP * BS), jnp.bfloat16),
                pltpu.VMEM((2, NEAR_E // 2 + 1, BS, LANES), jnp.float32),
                pltpu.VMEM((KA * BS // 2, LANES), jnp.float32),
            ],
        ),
        compiler_params=pltpu.CompilerParams(vmem_limit_bytes=60 * 2**20),
        cost_estimate=pl.CostEstimate(flops=10**10, bytes_accessed=16 * 2**20, transcendentals=0),
        name="near",
    )(cols, lists, counts, operator_blocks, *near_rows)


def far_call(half, cols, lists, counts, position, operator_blocks, far_rows, matched, left, n_dom):
    far_spec = lambda m: pl.BlockSpec((1, ROW_T, LANES), lambda i, cols, *_: (cols[i * KH + m], 0, 0))
    slot_shape = (HALF_C // 2 * BS, LANES)
    hbm = lambda x: pltpu.with_memory_space_constraint(x, pltpu.HBM)
    return pl.pallas_call(
        far_kernel,
        out_shape=tuple(jax.ShapeDtypeStruct((n,) + slot_shape, jnp.float32) for n in (8, 8, 8, 8, 1)),
        grid_spec=pltpu.PrefetchScalarGridSpec(
            num_scalar_prefetch=4,
            grid=(RB,),
            in_specs=[pl.BlockSpec((1, 8, BS * BS), lambda i, *_: (i, 1, 0))]
            + [far_spec(m) for m in range(KH)]
            + [
                pl.BlockSpec((1, KP, HALF_C // 2, BS, LANES), lambda i, *_: (i, 0, half, 0, 0)),
                pl.BlockSpec((1, KP, LANES, LANES), lambda i, *_: (i, 0, 0, 0)),
            ],
            out_specs=(pl.BlockSpec(memory_space=pltpu.HBM),) * 5,
            scratch_shapes=[
                pltpu.VMEM((KH, LANES, KP * BS), jnp.bfloat16),
                pltpu.VMEM((2, FAR_E // 2 + 1, BS, LANES), jnp.float32),
                pltpu.VMEM((2, LANES, HALF_C * BS), jnp.bfloat16),
                pltpu.VMEM((n_dom + 1,) + slot_shape, jnp.float32),
                pltpu.VMEM((8 * BS // 2, LANES), jnp.float32),
                pltpu.SemaphoreType.DMA((5,)),
            ],
        ),
        compiler_params=pltpu.CompilerParams(vmem_limit_bytes=40 * 2**20),
        cost_estimate=pl.CostEstimate(flops=5 * 10**9, bytes_accessed=14 * 2**20, transcendentals=0),
        name="far",
    )(cols, lists, counts, position, operator_blocks, *([far_rows] * KH), hbm(matched), hbm(left))


SIDE = 4


def places(device, me):
    x, y, k = device // (2 * SIDE), device // 2 % SIDE, device % 2
    return jnp.where(me % 2 == 0, x, y), jnp.where(me % 2 == 0, y, x), k


def device_at(u, v, k, me):
    u, v, k = u % SIDE, v % SIDE, k % 2
    return (jnp.where(me % 2 == 0, u, v) * SIDE + jnp.where(me % 2 == 0, v, u)) * 2 + k


def shift_pairs(shift, phase):
    pairs = []
    for x in range(SIDE):
        for y in range(SIDE):
            for k in range(2):
                along_x = (k == 0) == (phase == 0)
                to_x, to_y = ((x + shift) % SIDE, y) if along_x else (x, (y + shift) % SIDE)
                pairs.append(((x * SIDE + y) * 2 + k, (to_x * SIDE + to_y) * 2 + k))
    return pairs


def per_device(
    operator_blocks,
    operator_cols,
    halo_count,
    prolong_blocks,
    prolong_cols,
    prolong_slot,
    send_lists,
    slot_owner_row,
    coarse_pattern,
):
    n_dom = lax.axis_size("dom")
    n_grp = lax.axis_size("grp")
    g = lax.axis_index("grp")
    d = lax.axis_index("dom")
    owner = slot_owner_row.reshape(-1)

    outgoing, carried = pl.pallas_call(
        outgoing_kernel,
        out_shape=(
            jax.ShapeDtypeStruct((n_dom, ROW_T, LANES), jnp.float32),
            jax.ShapeDtypeStruct((RB * ROW_T + 8, LANES), jnp.float32),
        ),
        grid_spec=pltpu.PrefetchScalarGridSpec(
            num_scalar_prefetch=1,
            grid=(1,),
            in_specs=[
                pl.BlockSpec((RB, KP, BS * BS), lambda i, *_: (0, 0, 0)),
                pl.BlockSpec((RB, KP), lambda i, *_: (0, 0)),
            ],
            out_specs=(
                pl.BlockSpec(memory_space=pltpu.HBM),
                pl.BlockSpec((RB * ROW_T + 8, LANES), lambda i, *_: (0, 0)),
            ),
            scratch_shapes=[pltpu.VMEM((KP * BS // 2, LANES), jnp.float32), pltpu.SemaphoreType.DMA((n_dom,))],
        ),
        cost_estimate=pl.CostEstimate(flops=0, bytes_accessed=6 * 2**20, transcendentals=0),
        name="outgoing",
    )(send_lists.reshape(-1), prolong_blocks, prolong_cols)
    far_rows = lax.all_to_all(outgoing, "dom", split_axis=0, concat_axis=0, tiled=True)

    wide = lambda x: jnp.pad(x, ((0, 0), (0, 2 * n_dom - x.shape[1])))
    mine = jnp.concatenate([wide(prolong_cols), wide(coarse_pattern), wide(send_lists), slot_owner_row], axis=0)
    told = lax.all_to_all(
        jnp.broadcast_to(mine[None], (n_dom,) + mine.shape), "dom", split_axis=0, concat_axis=0, tiled=True
    )
    told, operator_cols, prolong_slot, halo_count, owner = lax.optimization_barrier(
        (told, operator_cols, prolong_slot, halo_count, owner)
    )
    all_cols = told[:, :RB, :KP]
    patterns = told[:, RB : RB + 2, :KC].reshape(2 * n_dom, KC)
    here = jnp.arange(2 * n_dom, dtype=jnp.int32)[None, :] == d
    picked = jnp.sum(jnp.where(here, told[:, RB + 2], 0), axis=1)
    slot_rows = told[:, RB + 3]
    far_ids = jnp.sum(
        jnp.where((picked[:, None] == jnp.arange(RB, dtype=jnp.int32))[:, :, None], all_cols, 0), axis=1
    )

    slots = prolong_slot.reshape(-1)
    slot_row = pick_rows(owner[:, None], slots)[:, 0]
    wanted = pick_rows(patterns, (slots // 2) * 2 + slot_row)
    u, v, k = places(d, d)
    to_u, to_v, to_k = places(slots // 2, d)
    position = ((to_u - u) % SIDE) * 8 + ((to_v - v) % SIDE) * 2 + (to_k - k) % 2
    position = jnp.where(slots % 2 == 1, n_dom, position)

    passed, _ = lax.optimization_barrier((carried, wanted))
    near_rows = [carried]
    for dz in range(1, n_grp):
        near_rows.append(lax.ppermute(passed, "grp", [((z + dz) % n_grp, z) for z in range(n_grp)]))

    near_ids_table = jnp.concatenate(
        [rows[RB * ROW_T : RB * ROW_T + RB, :KP].astype(jnp.int32) for rows in near_rows], axis=0
    )
    near_slots = operator_cols[:, :KG]
    near_cols = (((near_slots // RB) - g) % n_grp * RB + near_slots % RB).reshape(-1)
    far_cols = operator_cols[:, KG:].reshape(-1)
    near_ids = pick_rows(near_ids_table, near_cols).reshape(RB, NEAR_E)
    far_ids = pick_rows(far_ids, far_cols).reshape(RB, FAR_E)
    live = jnp.arange(KH, dtype=jnp.int32)[None, :] < halo_count[:, None]
    spread = lambda x: jnp.repeat(x, KP, axis=0)
    near_list, near_count = match_lists(wanted, spread(near_ids), jnp.ones((PAIRS, NEAR_E), bool))
    far_live = spread(jnp.repeat(live, KP, axis=1))
    far_lists = [
        match_lists(wanted[:, half * HALF_C : (half + 1) * HALF_C], spread(far_ids), far_live) for half in range(HALVES)
    ]

    matched, left = near_call(near_cols, near_list, near_count, operator_blocks, near_rows)
    slot_shape = (HALF_C // 2 * BS, LANES)
    sources = jnp.stack([device_at(u - t, v, k, d) for t in range(SIDE)])
    owners = jnp.stack([device_at(u, v + p // 2, k + p % 2, d) for p in range(8)])
    rows_from = pick_rows(slot_rows, sources)
    row_of = pick_rows(rows_from.T, 2 * owners).T
    two = jnp.arange(2, dtype=jnp.int32)
    second_row = (two == 1 - row_of[0, 0])[None] & (two == 0)[:, None]

    def first_phase(half):
        far_list, far_count = far_lists[half]
        chunks = far_call(
            half, far_cols, far_list, far_count, position, operator_blocks, far_rows, matched, left, n_dom
        )
        sent = {t: lax.ppermute(chunks[t], "dom", shift_pairs(t, 0)) for t in (1, 3, 2)}
        return lax.optimization_barrier((chunks[0], sent[1], sent[2], sent[3], chunks[4]))

    def second_phase(here):
        *arriving, second = here

        def owned(t2):
            total = 0.0
            for t in range(SIDE):
                part = arriving[t][2 * t2 : 2 * t2 + 2][:, None]
                to_row = row_of[t, 2 * t2 : 2 * t2 + 2][:, None] == two
                total = total + jnp.where(to_row[:, :, None, None], part, 0.0)
            if t2 == 0:
                total = total + jnp.where(second_row[:, :, None, None], second[:, None], 0.0)
            return total

        sent = [lax.ppermute(owned(t2), "dom", shift_pairs(t2, 1)) for t2 in (2, 1, 3)]
        return owned(0), sent

    def swap(kept, sent):
        sums = [kept[kk] + sent[1][kk] + sent[0][kk] + sent[2][kk] for kk in (1, 0)]
        return sums[1], lax.ppermute(sums[0], "dom", [(n, n ^ 1) for n in range(n_dom)])

    arrived = [first_phase(half) for half in range(HALVES)]
    halves = [second_phase(here) for here in arrived]
    parts = [swap(*half) for half in halves]

    row_spec = pl.BlockSpec((1,) + slot_shape, lambda i: (i, 0, 0))
    return pl.pallas_call(
        final_kernel,
        out_shape=jax.ShapeDtypeStruct((2, KC, BS * BS), jnp.float32),
        grid=(2,),
        in_specs=[row_spec] * (2 * HALVES),
        out_specs=pl.BlockSpec((1, KC, BS * BS), lambda i: (i, 0, 0)),
        scratch_shapes=[pltpu.VMEM((KC * BS // 2, LANES), jnp.float32)],
        compiler_params=pltpu.CompilerParams(vmem_limit_bytes=16 * 2**20),
        name="final",
    )(*[x for pair in parts for x in pair])


def solution(mesh):
    return jax.shard_map(
        per_device,
        mesh=mesh,
        in_specs=(
            P(("grp", "dom"), None, None),
            P(("grp", "dom"), None),
            P(("grp", "dom")),
            P(("grp", "dom"), None, None),
            P(("grp", "dom"), None),
            P(("grp", "dom"), None),
            P(("grp", "dom"), None),
            P(("grp", "dom"), None),
            P(("grp", "dom"), None),
        ),
        out_specs=P(("grp", "dom"), None, None),
        check_vma=False,
    )
```
